256 devices in a mesh: seq: 32 (over z, y), head: 8 (over x, core).
Axes of the slice: x: 4, y: 4, z: 8, core: 2. Of those that a mesh axis runs over, the one named last changes fastest.
Arguments:
- queries: bfloat16 [16384, 8192], P('seq', 'head'), may hold values from -6 to 6
- keys: bfloat16 [16384, 8192], P('seq', 'head'), may hold values from -6 to 6
- values: bfloat16 [16384, 8192], P('seq', 'head'), may hold values from -10 to 10
- norm_gain: float32 [8192], P('head'), may hold values from 0.1 to 1.9
- out_grad: bfloat16 [16384, 8192], P('seq', 'head'), may hold values from -6 to 6
Outputs:
- normed: bfloat16 [16384, 8192], P('seq', 'head')
- query_grad: bfloat16 [16384, 8192], P('seq', 'head')
- key_grad: bfloat16 [16384, 8192], P('seq', 'head')
- value_grad: bfloat16 [16384, 8192], P('seq', 'head')
The draws below stay inside these ranges and needn't reach their ends.
All inputs are finite; a program needn't handle non-finite values.
Results may differ from the reference program's by a relative error of at most 0.0058.
Values sent between devices are 32-bit elements; how exact they have to be, the bound alone decides.
A program may use at most 128 MiB of HBM per device.

```python
import jax
import jax.numpy as jnp
from jax import lax

HD = 128
BLK = 512
HEADS = 64
D = 8192
TOKENS = 16384


def draw_values(key, part):
    key = jax.random.fold_in(key, 11)
    noise_key, level_key = jax.random.split(key, 2)
    heads_index = jnp.arange(D) // HD
    ramp = jnp.exp(0.7 * heads_index.astype(jnp.float32) / max(HEADS - 1, 1))
    jitter = jax.random.uniform(level_key, (HEADS,), jnp.float32, 0.85, 1.15)
    level = ramp * jitter[heads_index]
    base = jnp.clip(jax.random.normal(noise_key, (TOKENS, D), jnp.float32), -4.0, 4.0)
    return jnp.clip(base * level[None, :], -9.5, 9.5).astype(jnp.bfloat16)


def level_of(rng, extent, pieces, least, high):
    level, own = 1.0, jax.random.fold_in(rng, 6)
    for position, shards_of in pieces:
        heights = jnp.exp(jax.random.uniform(jax.random.fold_in(own, position), (shards_of,), jnp.float32, least / len(pieces), high / len(pieces)))
        level = level * jnp.repeat(heights, extent[position] // shards_of).reshape([-1 if axis == position else 1 for axis in range(len(extent))])
    return level


def normal_values(own_key, shape, width, bound, shards=(), kind=jnp.bfloat16):
    array = jax.random.normal(own_key, shape, jnp.float32) * width
    if len(shards) > 0:
        array = level_of(own_key, shape, shards, -0.22, 0.18) * array
    return jnp.clip(array, min=-bound, max=bound).astype(kind)


def setup_inputs(seed: int = 0) -> dict:
    streams_of = jax.random.split(jax.random.key(seed), 6)
    return {
        "queries": normal_values(streams_of[0], (TOKENS, D), 1.0, 6.0, ((0, 32), (1, 8))),
        "keys": normal_values(streams_of[1], (TOKENS, D), 1.0, 6.0, ((0, 32), (1, 8))),
        "values": draw_values(jax.random.fold_in(streams_of[5], 71), 0),
        "norm_gain": jnp.clip(1.0 + 0.18 * jax.random.normal(streams_of[3], (D,), jnp.float32), 0.1, 1.9),
        "out_grad": normal_values(streams_of[4], (TOKENS, D), 1.0, 6.0, ((0, 32), (1, 8))),
    }


def reference(queries, keys, values, norm_gain, out_grad):
    total_tok = queries.shape[0]
    count = total_tok // BLK
    scale = HD ** (-0.5)
    lower = jnp.tril(jnp.ones((BLK, BLK), dtype=bool))
    shape4 = (count, BLK, HEADS, HD)
    query_b = queries.reshape(shape4)
    key_b = keys.reshape(shape4)
    value_b = values.reshape(shape4)
    grad_b = out_grad.reshape((count, BLK, D))
    gain = norm_gain.astype(jnp.float32)

    def forward(carry, blocks):
        query, key, value, grad = blocks
        query = query.astype(jnp.float32)
        key = key.astype(jnp.float32)
        value = value.astype(jnp.float32)
        state_bf = carry.astype(jnp.bfloat16)
        raw = jnp.einsum('thd,shd->hts', query, key) * scale
        scores = jnp.where(lower[None], raw, 0.0).astype(jnp.bfloat16)
        attended = jnp.einsum('hts,she->the', scores.astype(jnp.float32), value)
        attended = attended + scale * jnp.einsum('thd,hde->the', query, state_bf.astype(jnp.float32))
        flat = attended.reshape(BLK, D)
        rms = jnp.sqrt(lax.optimization_barrier(jnp.sum(flat * flat, axis=1, keepdims=True)) / D + 1e-06)
        unit = flat / rms
        normed = (unit * gain).astype(jnp.bfloat16)
        grad_norm = grad.astype(jnp.float32) * gain
        proj = lax.optimization_barrier(jnp.sum(grad_norm * unit, axis=1, keepdims=True)) / D
        att_grad = ((grad_norm - unit * proj) / rms).astype(jnp.bfloat16)
        carry = carry + jnp.einsum('shd,she->hde', key, value)
        return (carry, (normed, att_grad, state_bf))
    zero = jnp.zeros((HEADS, HD, HD), jnp.float32)
    _, (normed, att_grad, states) = lax.scan(forward, zero, (query_b, key_b, value_b, grad_b))
    att_grad4 = att_grad.reshape(shape4)

    def backward(carry, blocks):
        query, key, value, agrad, state_bf = blocks
        query = query.astype(jnp.float32)
        key = key.astype(jnp.float32)
        value = value.astype(jnp.float32)
        agrad = agrad.astype(jnp.float32)
        state_f = state_bf.astype(jnp.float32)
        later = carry.astype(jnp.bfloat16).astype(jnp.float32)
        raw = jnp.einsum('thd,shd->hts', query, key) * scale
        scores = jnp.where(lower[None], raw, 0.0).astype(jnp.bfloat16).astype(jnp.float32)
        graw = jnp.einsum('the,she->hts', agrad, value)
        gscores = jnp.where(lower[None], graw, 0.0).astype(jnp.bfloat16).astype(jnp.float32)
        qgrad = scale * (jnp.einsum('hts,shd->thd', gscores, key) + jnp.einsum('the,hde->thd', agrad, state_f))
        kgrad = scale * (jnp.einsum('hts,thd->shd', gscores, query) + jnp.einsum('she,hde->shd', value, later))
        vgrad = jnp.einsum('hts,the->she', scores, agrad) + scale * jnp.einsum('shd,hde->she', key, later)
        carry = carry + jnp.einsum('thd,the->hde', query, agrad)
        return (carry, (qgrad.astype(jnp.bfloat16), kgrad.astype(jnp.bfloat16), vgrad.astype(jnp.bfloat16)))
    _, (qgrads, kgrads, vgrads) = lax.scan(backward, zero, (query_b, key_b, value_b, att_grad4, states), reverse=True)
    return (normed.reshape(total_tok, D), qgrads.reshape(total_tok, D), kgrads.reshape(total_tok, D), vgrads.reshape(total_tok, D))
```

```python
import functools

import jax
import jax.numpy as jnp
from jax import lax
from jax.experimental import pallas as pl
from jax.experimental.pallas import tpu as pltpu
from jax.sharding import PartitionSpec as P

HD = 128
BLK = 512
NY = 4
CHUNKS = 2
HALF = BLK // 2
F32 = jnp.float32
BF16 = jnp.bfloat16
MESH = pl.DeviceIdType.MESH
EXACT = lax.Precision.HIGHEST


def dot_nn(a, b):
    return lax.dot_general(a, b, (((1,), (0,)), ((), ())), preferred_element_type=F32)


def dot_nt(a, b):
    return lax.dot_general(a, b, (((1,), (1,)), ((), ())), preferred_element_type=F32)


def dot_tn(a, b):
    return lax.dot_general(a, b, (((0,), (0,)), ((), ())), preferred_element_type=F32)


def exact_nt(a, b):
    return lax.dot_general(a, b, (((1,), (1,)), ((), ())), precision=EXACT, preferred_element_type=F32)


def exact_tn(a, b):
    return lax.dot_general(a, b, (((0,), (0,)), ((), ())), precision=EXACT, preferred_element_type=F32)


class Scan:
    def __init__(self, nz, rows, reverse, refs, sems):
        self.nz, self.rows, self.reverse = nz, rows, reverse
        self.block, self.b1, self.tot, self.b2, self.pre, self.b3, self.ret, self.b4 = refs
        self.ysend, self.yrecv, self.zsend, self.zrecv = sems
        seq = lax.axis_index("seq")
        self.head = lax.axis_index("head")
        self.z, self.y = lax.div(seq, NY), lax.rem(seq, NY)
        self.quarter = rows // NY
        self.piece = self.quarter // nz
        self.sends = []

    def y_copy(self, phase, c, d, src, dst):
        k = (phase * CHUNKS + c) * (NY - 1) + d - 1
        to = self.z * NY + lax.rem(self.y + d, NY)
        return pltpu.make_async_remote_copy(
            src_ref=src, dst_ref=dst, send_sem=self.ysend.at[k], recv_sem=self.yrecv.at[k],
            device_id=(to, self.head), device_id_type=MESH,
        )

    def z_copy(self, phase, c, d, src, dst):
        k = (phase * CHUNKS + c) * (self.nz - 1) + d - 1
        to = lax.rem(self.z + d, self.nz) * NY + self.y
        return pltpu.make_async_remote_copy(
            src_ref=src, dst_ref=dst, send_sem=self.zsend.at[k], recv_sem=self.zrecv.at[k],
            device_id=(to, self.head), device_id_type=MESH,
        )

    def begin(self, copies):
        for copy in copies:
            copy.start()
        self.sends += copies
        return copies

    def y_out(self, c):
        base = c * self.rows

        def part(q):
            return self.block.at[pl.ds(pl.multiple_of(base + q * self.quarter, 8), self.quarter)]

        copies = self.begin([
            self.y_copy(0, c, d, part(lax.rem(self.y + d, NY)), self.b1.at[c, self.y]) for d in (2, 1, 3)
        ])
        self.b1[c, self.y] = part(self.y)[...]
        return copies

    def z_out(self, c, arriving):
        for copy in arriving:
            copy.wait_recv()
        self.tot[c] = (self.b1[c, 0] + self.b1[c, 1]) + (self.b1[c, 2] + self.b1[c, 3])

        def part(j):
            return self.tot.at[c, pl.ds(pl.multiple_of(j * self.piece, 8), self.piece)]

        far = sorted(range(1, self.nz), key=lambda d: -min(d, self.nz - d))
        copies = self.begin([
            self.z_copy(0, c, d, part(lax.rem(self.z + d, self.nz)), self.b2.at[c, self.z]) for d in far
        ])
        self.b2[c, self.z] = part(self.z)[...]
        return copies

    def z_back(self, c, arriving):
        for copy in arriving:
            copy.wait_recv()
        order = range(self.nz)
        total = jnp.zeros((self.piece, HD), F32)
        for j in reversed(order) if self.reverse else order:
            self.pre[c, j] = total
            total = total + self.b2[c, j]
        far = sorted(range(1, self.nz), key=lambda d: -min(d, self.nz - d))
        copies = self.begin([
            self.z_copy(1, c, d, self.pre.at[c, lax.rem(self.z + d, self.nz)], self.b3.at[c, self.z]) for d in far
        ])
        self.b3[c, self.z] = self.pre[c, self.z]
        return copies

    def y_back(self, c, arriving):
        for copy in arriving:
            copy.wait_recv()
        total = self.b3[c].reshape(self.quarter, HD)
        order = range(NY)
        for j in reversed(order) if self.reverse else order:
            self.ret[c, j] = total
            total = total + self.b1[c, j]
        copies = self.begin([
            self.y_copy(1, c, d, self.ret.at[c, lax.rem(self.y + d, NY)], self.b4.at[c, self.y]) for d in (2, 1, 3)
        ])
        self.b4[c, self.y] = self.ret[c, self.y]
        return copies

    def finish(self):
        for copy in self.sends:
            copy.wait_send()


def kernel(nz, nh, heads, q_hbm, k_hbm, v_hbm, gain_hbm, g_hbm, normed_hbm, qgrad_hbm, kgrad_hbm, vgrad_hbm,
           q, k, v, gain, g, scores, att, dout, kpart, vpart, normed, qgrad, kgrad, vgrad, state_bf, squares,
           products, inv_b, coef_b, head_src, head_dst, *rest):
    fwd_refs, bwd_refs = rest[0:8], rest[8:16]
    fwd_sems, bwd_sems = rest[16:20], rest[20:24]
    in_sem, out_sem, head_send, head_recv = rest[24:28]
    later_bf = rest[28]
    scale = HD ** (-0.5)
    per = heads // CHUNKS
    rows = per * HD
    width = heads * HD
    seq, head = lax.axis_index("seq"), lax.axis_index("head")
    z, y = lax.div(seq, NY), lax.rem(seq, NY)

    barrier = pltpu.get_barrier_semaphore()
    for d in range(1, NY):
        to = z * NY + lax.rem(y + d, NY)
        pl.semaphore_signal(barrier, inc=1, device_id=(to, head), device_id_type=MESH)
    for d in range(1, nz):
        to = lax.rem(z + d, nz) * NY + y
        pl.semaphore_signal(barrier, inc=1, device_id=(to, head), device_id_type=MESH)
    for d in range(1, nh):
        pl.semaphore_signal(barrier, inc=1, device_id=(seq, lax.rem(head + d, nh)), device_id_type=MESH)

    loads = []
    for c in range(CHUNKS):
        cols = pl.ds(c * rows, rows)
        pair = []
        for i, (src, dst) in enumerate(((k_hbm, k), (v_hbm, v))):
            copy = pltpu.make_async_copy(src.at[:, cols], dst.at[:, cols], in_sem.at[2 * c + i])
            copy.start()
            pair.append(copy)
        loads.append(pair)
    late = []
    for i, (src, dst) in enumerate(((q_hbm, q), (g_hbm, g), (gain_hbm, gain))):
        copy = pltpu.make_async_copy(src, dst, in_sem.at[2 * CHUNKS + i])
        copy.start()
        late.append(copy)

    fwd = Scan(nz, rows, False, fwd_refs, fwd_sems)
    bwd = Scan(nz, rows, True, bwd_refs, bwd_sems)

    def lanes(h):
        return pl.ds(pl.multiple_of(h * HD, HD), HD)

    def sub(h):
        return pl.ds(pl.multiple_of(h * HD, HD), HD)

    def each(first, count, body):
        def step(h, _):
            body(h)
            return 0

        lax.fori_loop(first, first + count, step, 0)

    def kv(h):
        fwd.block[sub(h), :] = dot_tn(k[:, lanes(h)], v[:, lanes(h)])

    moving = []
    for c in range(CHUNKS):
        for copy in loads[c]:
            copy.wait()
        each(c * per, per, kv)
        if c == 0:
            pl.semaphore_wait(barrier, (NY - 1) + (nz - 1) + (nh - 1))
        moving.append(fwd.y_out(c))
    for copy in late:
        copy.wait()

    causal = lax.broadcasted_iota(jnp.int32, (HALF, HALF), 0) >= lax.broadcasted_iota(jnp.int32, (HALF, HALF), 1)

    def tiles(a, b, factor):
        top = jnp.where(causal, dot_nt(a[:HALF], b[:HALF]) * factor, 0.0).astype(BF16)
        low = (dot_nt(a[HALF:], b[:HALF]) * factor).astype(BF16)
        end = jnp.where(causal, dot_nt(a[HALF:], b[HALF:]) * factor, 0.0).astype(BF16)
        return top, low, end

    def intra(h):
        vh = v[:, lanes(h)]
        top, low, end = tiles(q[:, lanes(h)], k[:, lanes(h)], scale)
        scores[h, 0], scores[h, 1], scores[h, 2] = top, low, end
        att[:HALF, lanes(h)] = dot_nn(top, vh[:HALF])
        att[HALF:, lanes(h)] = dot_nn(low, vh[:HALF]) + dot_nn(end, vh[HALF:])

    each(0, heads // 2, intra)
    for c in range(CHUNKS):
        moving[c] = fwd.z_out(c, moving[c])
    each(heads // 2, heads - heads // 2, intra)
    for c in range(CHUNKS):
        moving[c] = fwd.z_back(c, moving[c])
    squares[...] = jnp.zeros_like(squares)
    products[...] = jnp.zeros_like(products)
    for c in range(CHUNKS):
        moving[c] = fwd.y_back(c, moving[c])

    for c in range(CHUNKS):
        for copy in moving[c]:
            copy.wait_recv()
        state_bf[pl.ds(c * rows, rows), :] = fwd.b4[c].reshape(rows, HD).astype(BF16)

        def attend(h):
            a = att[:, lanes(h)] + scale * dot_nn(q[:, lanes(h)], state_bf[sub(h), :])
            att[:, lanes(h)] = a
            squares[...] += a * a
            products[...] += a * (g[:, lanes(h)].astype(F32) * gain[:, lanes(h)])

        each(c * per, per, attend)

    row = lax.broadcasted_iota(jnp.int32, (8, HD), 0)
    groups = BLK // HD
    packed = jnp.zeros((8, HD), F32)
    for t in range(groups):
        part = pl.ds(t * HD, HD)
        packed = packed + exact_nt((row == t).astype(F32), squares[part, :])
        packed = packed + exact_nt((row == groups + t).astype(F32), products[part, :])
    head_src[...] = packed
    head_copies = []
    for d in range(1, nh):
        copy = pltpu.make_async_remote_copy(
            src_ref=head_src, dst_ref=head_dst.at[head], send_sem=head_send.at[d - 1], recv_sem=head_recv.at[d - 1],
            device_id=(seq, lax.rem(head + d, nh)), device_id_type=MESH,
        )
        copy.start()
        head_copies.append(copy)
    head_dst[head] = packed
    for copy in head_copies:
        copy.wait_recv()
    sums = head_dst[0]
    for j in range(1, nh):
        sums = sums + head_dst[j]
    full = nh * width
    inv = 1.0 / jnp.sqrt(sums[:groups] / full + 1e-06)
    proj = (sums[groups:] * inv) / full
    both = jnp.concatenate([inv, (inv * proj) * inv], axis=0)
    for t in range(groups):
        part = pl.ds(t * HD, HD)
        inv_b[part, :] = exact_tn(both, (row == t).astype(F32))
        coef_b[part, :] = exact_tn(both, (row == groups + t).astype(F32))

    def grad(h):
        gn = g[:, lanes(h)].astype(F32) * gain[:, lanes(h)]
        d = (gn * inv_b[...] - att[:, lanes(h)] * coef_b[...]).astype(BF16)
        dout[:, lanes(h)] = d
        bwd.block[sub(h), :] = dot_tn(q[:, lanes(h)], d)

    for c in range(CHUNKS):
        each(c * per, per, grad)
        moving[c] = bwd.y_out(c)

    def back(h):
        qh, kh, vh, d = q[:, lanes(h)], k[:, lanes(h)], v[:, lanes(h)], dout[:, lanes(h)]
        normed[:, lanes(h)] = (att[:, lanes(h)] * inv_b[...] * gain[:, lanes(h)]).astype(BF16)
        top, low, end = tiles(d, vh, 1.0)
        carried = dot_nt(d, state_bf[sub(h), :])
        qgrad[:HALF, lanes(h)] = (scale * (dot_nn(top, kh[:HALF]) + carried[:HALF])).astype(BF16)
        qgrad[HALF:, lanes(h)] = (
            scale * (dot_nn(low, kh[:HALF]) + dot_nn(end, kh[HALF:]) + carried[HALF:])
        ).astype(BF16)
        kpart[:HALF, lanes(h)] = dot_tn(top, qh[:HALF]) + dot_tn(low, qh[HALF:])
        kpart[HALF:, lanes(h)] = dot_tn(end, qh[HALF:])
        vpart[:HALF, lanes(h)] = dot_tn(scores[h, 0], d[:HALF]) + dot_tn(scores[h, 1], d[HALF:])
        vpart[HALF:, lanes(h)] = dot_tn(scores[h, 2], d[HALF:])

    outs = []

    def put(src, dst):
        copy = pltpu.make_async_copy(src, dst, out_sem.at[len(outs)])
        copy.start()
        outs.append(copy)

    each(0, heads // 2, back)
    for c in range(CHUNKS):
        moving[c] = bwd.z_out(c, moving[c])
    each(heads // 2, heads - heads // 2, back)
    for c in range(CHUNKS):
        moving[c] = bwd.z_back(c, moving[c])
    put(normed, normed_hbm)
    put(qgrad, qgrad_hbm)
    for c in range(CHUNKS):
        moving[c] = bwd.y_back(c, moving[c])
    for c in range(CHUNKS):
        for copy in moving[c]:
            copy.wait_recv()

        def last(h):
            here = later_bf[sub(h), :]
            kgrad[:, lanes(h)] = (scale * (kpart[:, lanes(h)] + dot_nt(v[:, lanes(h)], here))).astype(BF16)
            vgrad[:, lanes(h)] = (vpart[:, lanes(h)] + scale * dot_nn(k[:, lanes(h)], here)).astype(BF16)

        later_bf[pl.ds(c * rows, rows), :] = bwd.b4[c].reshape(rows, HD).astype(BF16)
        each(c * per, per, last)
        cols = pl.ds(c * rows, rows)
        put(kgrad.at[:, cols], kgrad_hbm.at[:, cols])
        put(vgrad.at[:, cols], vgrad_hbm.at[:, cols])

    fwd.finish()
    for copy in head_copies:
        copy.wait_send()
    bwd.finish()
    for copy in outs:
        copy.wait()


def local(queries, keys, values, norm_gain, out_grad):
    blk, width = queries.shape
    heads = width // HD
    nz = lax.axis_size("seq") // NY
    nh = lax.axis_size("head")
    rows = heads // CHUNKS * HD
    quarter = rows // NY
    piece = quarter // nz
    vmem = pltpu.VMEM

    def scan_refs():
        return [
            vmem((heads * HD, HD), F32),
            vmem((CHUNKS, NY, quarter, HD), F32),
            vmem((CHUNKS, quarter, HD), F32),
            vmem((CHUNKS, nz, piece, HD), F32),
            vmem((CHUNKS, nz, piece, HD), F32),
            vmem((CHUNKS, nz, piece, HD), F32),
            vmem((CHUNKS, NY, quarter, HD), F32),
            vmem((CHUNKS, NY, quarter, HD), F32),
        ]

    def scan_sems():
        y, zz = 2 * CHUNKS * (NY - 1), 2 * CHUNKS * (nz - 1)
        dma = pltpu.SemaphoreType.DMA
        return [dma((y,)), dma((y,)), dma((zz,)), dma((zz,))]

    big_f32, big_bf16 = vmem((blk, width), F32), vmem((blk, width), BF16)
    scratch = [
        big_bf16, big_bf16, big_bf16, vmem((1, width), F32), big_bf16,
        vmem((heads, 3, HALF, HALF), BF16),
        big_f32, big_bf16, big_f32, big_f32,
        big_bf16, big_bf16, big_bf16, big_bf16,
        vmem((heads * HD, HD), BF16),
        vmem((blk, HD), F32), vmem((blk, HD), F32), vmem((blk, HD), F32), vmem((blk, HD), F32),
        vmem((8, HD), F32), vmem((nh, 8, HD), F32),
        *scan_refs(), *scan_refs(), *scan_sems(), *scan_sems(),
        pltpu.SemaphoreType.DMA((2 * CHUNKS + 3,)),
        pltpu.SemaphoreType.DMA((2 + 2 * CHUNKS,)),
        pltpu.SemaphoreType.DMA((nh - 1,)),
        pltpu.SemaphoreType.DMA((nh - 1,)),
        vmem((heads * HD, HD), BF16),
    ]
    out = jax.ShapeDtypeStruct((blk, width), BF16)
    return pl.pallas_call(
        functools.partial(kernel, nz, nh, heads),
        out_shape=(out, out, out, out),
        in_specs=[pl.BlockSpec(memory_space=pl.ANY)] * 5,
        out_specs=(pl.BlockSpec(memory_space=pl.ANY),) * 4,
        scratch_shapes=scratch,
        compiler_params=pltpu.CompilerParams(
            collective_id=0, has_side_effects=True, vmem_limit_bytes=56 * 1024 * 1024
        ),
        name="linear_attention",
    )(queries, keys, values, norm_gain.reshape(1, width), out_grad)


def solution(mesh):
    placed = (P("seq", "head"), P("seq", "head"), P("seq", "head"), P("head"), P("seq", "head"))
    return jax.shard_map(
        local,
        mesh=mesh,
        in_specs=placed,
        out_specs=(P("seq", "head"), P("seq", "head"), P("seq", "head"), P("seq", "head")),
        check_vma=False,
    )
```

```python
import functools

import jax
import jax.numpy as jnp
from jax import lax
from jax.experimental import pallas as pl
from jax.experimental.pallas import tpu as pltpu
from jax.sharding import PartitionSpec as P

HD = 128
BLK = 512
NY = 4
CHUNKS = 4
LAST = 4
HALF = BLK // 2
F32 = jnp.float32
BF16 = jnp.bfloat16
MESH = pl.DeviceIdType.MESH
EXACT = lax.Precision.HIGHEST


def dot_nn(a, b):
    return lax.dot_general(a, b, (((1,), (0,)), ((), ())), preferred_element_type=F32)


def dot_nt(a, b):
    return lax.dot_general(a, b, (((1,), (1,)), ((), ())), preferred_element_type=F32)


def dot_tn(a, b):
    return lax.dot_general(a, b, (((0,), (0,)), ((), ())), preferred_element_type=F32)


def exact_nt(a, b):
    return lax.dot_general(a, b, (((1,), (1,)), ((), ())), precision=EXACT, preferred_element_type=F32)


def exact_tn(a, b):
    return lax.dot_general(a, b, (((0,), (0,)), ((), ())), precision=EXACT, preferred_element_type=F32)


class Scan:
    def __init__(self, nz, rows, reverse, refs, sems):
        self.nz, self.rows, self.reverse = nz, rows, reverse
        self.block, self.b1, self.tot, self.b2, self.pre, self.b3, self.ret, self.b4 = refs
        self.ysend, self.yrecv, self.zsend, self.zrecv = sems
        seq = lax.axis_index("seq")
        self.head = lax.axis_index("head")
        self.z, self.y = lax.div(seq, NY), lax.rem(seq, NY)
        self.quarter = rows // NY
        self.piece = self.quarter // nz
        self.sends = []

    def y_copy(self, phase, c, d, src, dst):
        k = (phase * CHUNKS + c) * (NY - 1) + d - 1
        to = self.z * NY + lax.rem(self.y + d, NY)
        return pltpu.make_async_remote_copy(
            src_ref=src, dst_ref=dst, send_sem=self.ysend.at[k], recv_sem=self.yrecv.at[k],
            device_id=(to, self.head), device_id_type=MESH,
        )

    def z_copy(self, phase, c, d, src, dst):
        k = (phase * CHUNKS + c) * (self.nz - 1) + d - 1
        to = lax.rem(self.z + d, self.nz) * NY + self.y
        return pltpu.make_async_remote_copy(
            src_ref=src, dst_ref=dst, send_sem=self.zsend.at[k], recv_sem=self.zrecv.at[k],
            device_id=(to, self.head), device_id_type=MESH,
        )

    def begin(self, copies):
        for copy in copies:
            copy.start()
        self.sends += copies
        return copies

    def y_out(self, c):
        base = c * self.rows

        def part(q):
            return self.block.at[pl.ds(pl.multiple_of(base + q * self.quarter, 8), self.quarter)]

        copies = self.begin([
            self.y_copy(0, c, d, part(lax.rem(self.y + d, NY)), self.b1.at[c, self.y]) for d in (2, 1, 3)
        ])
        self.b1[c, self.y] = part(self.y)[...]
        return copies

    def z_out(self, c, arriving):
        for copy in arriving:
            copy.wait_recv()
        self.tot[c] = (self.b1[c, 0] + self.b1[c, 1]) + (self.b1[c, 2] + self.b1[c, 3])

        def part(j):
            return self.tot.at[c, pl.ds(pl.multiple_of(j * self.piece, 8), self.piece)]

        far = sorted(range(1, self.nz), key=lambda d: -min(d, self.nz - d))
        copies = self.begin([
            self.z_copy(0, c, d, part(lax.rem(self.z + d, self.nz)), self.b2.at[c, self.z]) for d in far
        ])
        self.b2[c, self.z] = part(self.z)[...]
        return copies

    def z_back(self, c, arriving):
        for copy in arriving:
            copy.wait_recv()
        order = range(self.nz)
        total = jnp.zeros((self.piece, HD), F32)
        for j in reversed(order) if self.reverse else order:
            self.pre[c, j] = total
            total = total + self.b2[c, j]
        far = sorted(range(1, self.nz), key=lambda d: -min(d, self.nz - d))
        copies = self.begin([
            self.z_copy(1, c, d, self.pre.at[c, lax.rem(self.z + d, self.nz)], self.b3.at[c, self.z]) for d in far
        ])
        self.b3[c, self.z] = self.pre[c, self.z]
        return copies

    def y_back(self, c, arriving):
        for copy in arriving:
            copy.wait_recv()
        total = self.b3[c].reshape(self.quarter, HD)
        order = range(NY)
        for j in reversed(order) if self.reverse else order:
            self.ret[c, j] = total
            total = total + self.b1[c, j]
        copies = self.begin([
            self.y_copy(1, c, d, self.ret.at[c, lax.rem(self.y + d, NY)], self.b4.at[c, self.y]) for d in (2, 1, 3)
        ])
        self.b4[c, self.y] = self.ret[c, self.y]
        return copies

    def finish(self):
        for copy in self.sends:
            copy.wait_send()


def lanes(h):
    return pl.ds(pl.multiple_of(h * HD, HD), HD)


def sub(h):
    return pl.ds(pl.multiple_of(h * HD, HD), HD)


def each(first, count, body):
    def step(h, _):
        body(h)
        return 0

    lax.fori_loop(first, first + count, step, 0)


def kernel(nz, nh, heads, q_hbm, k_hbm, v_hbm, gain_hbm, g_hbm, normed, qgrad, kpart, vpart, later_bf, k, v,
           q, gain, g, scores, att, dout, state_bf, squares,
           products, inv_b, coef_b, head_src, head_dst, *rest):
    fwd_refs, bwd_refs = rest[0:8], rest[8:16]
    fwd_sems, bwd_sems = rest[16:20], rest[20:24]
    in_sem, head_send, head_recv = rest[24:27]
    scale = HD ** (-0.5)
    per = heads // CHUNKS
    rows = per * HD
    width = heads * HD
    seq, head = lax.axis_index("seq"), lax.axis_index("head")
    z, y = lax.div(seq, NY), lax.rem(seq, NY)

    barrier = pltpu.get_barrier_semaphore()
    for d in range(1, NY):
        to = z * NY + lax.rem(y + d, NY)
        pl.semaphore_signal(barrier, inc=1, device_id=(to, head), device_id_type=MESH)
    for d in range(1, nz):
        to = lax.rem(z + d, nz) * NY + y
        pl.semaphore_signal(barrier, inc=1, device_id=(to, head), device_id_type=MESH)
    for d in range(1, nh):
        pl.semaphore_signal(barrier, inc=1, device_id=(seq, lax.rem(head + d, nh)), device_id_type=MESH)

    loads = []
    for c in range(CHUNKS):
        cols = pl.ds(c * rows, rows)
        pair = []
        for i, (src, dst) in enumerate(((k_hbm, k), (v_hbm, v))):
            copy = pltpu.make_async_copy(src.at[:, cols], dst.at[:, cols], in_sem.at[2 * c + i])
            copy.start()
            pair.append(copy)
        loads.append(pair)
    late = []
    for i, (src, dst) in enumerate(((q_hbm, q), (g_hbm, g), (gain_hbm, gain))):
        copy = pltpu.make_async_copy(src, dst, in_sem.at[2 * CHUNKS + i])
        copy.start()
        late.append(copy)

    fwd = Scan(nz, rows, False, fwd_refs, fwd_sems)
    bwd = Scan(nz, rows, True, bwd_refs, bwd_sems)

    def kv(h):
        fwd.block[sub(h), :] = dot_tn(k[:, lanes(h)], v[:, lanes(h)])

    moving = []
    for c in range(CHUNKS):
        for copy in loads[c]:
            copy.wait()
        each(c * per, per, kv)
        if c == 0:
            pl.semaphore_wait(barrier, (NY - 1) + (nz - 1) + (nh - 1))
        moving.append(fwd.y_out(c))
    for copy in late:
        copy.wait()

    causal = lax.broadcasted_iota(jnp.int32, (HALF, HALF), 0) >= lax.broadcasted_iota(jnp.int32, (HALF, HALF), 1)

    def tiles(a, b, factor):
        top = jnp.where(causal, dot_nt(a[:HALF], b[:HALF]) * factor, 0.0).astype(BF16)
        low = (dot_nt(a[HALF:], b[:HALF]) * factor).astype(BF16)
        end = jnp.where(causal, dot_nt(a[HALF:], b[HALF:]) * factor, 0.0).astype(BF16)
        return top, low, end

    def intra(h):
        vh = v[:, lanes(h)]
        top, low, end = tiles(q[:, lanes(h)], k[:, lanes(h)], scale)
        scores[h, 0], scores[h, 1], scores[h, 2] = top, low, end
        att[:HALF, lanes(h)] = dot_nn(top, vh[:HALF])
        att[HALF:, lanes(h)] = dot_nn(low, vh[:HALF]) + dot_nn(end, vh[HALF:])

    each(0, heads // 2, intra)
    for c in range(CHUNKS):
        moving[c] = fwd.z_out(c, moving[c])
    each(heads // 2, heads - heads // 2, intra)
    for c in range(CHUNKS):
        moving[c] = fwd.z_back(c, moving[c])
    squares[...] = jnp.zeros_like(squares)
    products[...] = jnp.zeros_like(products)
    for c in range(CHUNKS):
        moving[c] = fwd.y_back(c, moving[c])

    for c in range(CHUNKS):
        for copy in moving[c]:
            copy.wait_recv()
        state_bf[pl.ds(c * rows, rows), :] = fwd.b4[c].reshape(rows, HD).astype(BF16)

        def attend(h):
            a = att[:, lanes(h)] + scale * dot_nn(q[:, lanes(h)], state_bf[sub(h), :])
            att[:, lanes(h)] = a
            squares[...] += a * a
            products[...] += a * (g[:, lanes(h)].astype(F32) * gain[:, lanes(h)])

        each(c * per, per, attend)

    row = lax.broadcasted_iota(jnp.int32, (8, HD), 0)
    groups = BLK // HD
    packed = jnp.zeros((8, HD), F32)
    for t in range(groups):
        part = pl.ds(t * HD, HD)
        packed = packed + exact_nt((row == t).astype(F32), squares[part, :])
        packed = packed + exact_nt((row == groups + t).astype(F32), products[part, :])
    head_src[...] = packed
    head_copies = []
    for d in range(1, nh):
        copy = pltpu.make_async_remote_copy(
            src_ref=head_src, dst_ref=head_dst.at[head], send_sem=head_send.at[d - 1], recv_sem=head_recv.at[d - 1],
            device_id=(seq, lax.rem(head + d, nh)), device_id_type=MESH,
        )
        copy.start()
        head_copies.append(copy)
    head_dst[head] = packed
    for copy in head_copies:
        copy.wait_recv()
    sums = head_dst[0]
    for j in range(1, nh):
        sums = sums + head_dst[j]
    full = nh * width
    inv = 1.0 / jnp.sqrt(sums[:groups] / full + 1e-06)
    proj = (sums[groups:] * inv) / full
    both = jnp.concatenate([inv, (inv * proj) * inv], axis=0)
    for t in range(groups):
        part = pl.ds(t * HD, HD)
        inv_b[part, :] = exact_tn(both, (row == t).astype(F32))
        coef_b[part, :] = exact_tn(both, (row == groups + t).astype(F32))

    def grad(h):
        gn = g[:, lanes(h)].astype(F32) * gain[:, lanes(h)]
        d = (gn * inv_b[...] - att[:, lanes(h)] * coef_b[...]).astype(BF16)
        dout[:, lanes(h)] = d
        bwd.block[sub(h), :] = dot_tn(q[:, lanes(h)], d)

    for c in range(CHUNKS):
        each(c * per, per, grad)
        moving[c] = bwd.y_out(c)

    def back(h):
        qh, kh, vh, d = q[:, lanes(h)], k[:, lanes(h)], v[:, lanes(h)], dout[:, lanes(h)]
        normed[:, lanes(h)] = (att[:, lanes(h)] * inv_b[...] * gain[:, lanes(h)]).astype(BF16)
        top, low, end = tiles(d, vh, 1.0)
        carried = dot_nt(d, state_bf[sub(h), :])
        qgrad[:HALF, lanes(h)] = (scale * (dot_nn(top, kh[:HALF]) + carried[:HALF])).astype(BF16)
        qgrad[HALF:, lanes(h)] = (
            scale * (dot_nn(low, kh[:HALF]) + dot_nn(end, kh[HALF:]) + carried[HALF:])
        ).astype(BF16)
        kpart[:HALF, lanes(h)] = dot_tn(top, qh[:HALF]) + dot_tn(low, qh[HALF:])
        kpart[HALF:, lanes(h)] = dot_tn(end, qh[HALF:])
        vpart[:HALF, lanes(h)] = dot_tn(scores[h, 0], d[:HALF]) + dot_tn(scores[h, 1], d[HALF:])
        vpart[HALF:, lanes(h)] = dot_tn(scores[h, 2], d[HALF:])

    each(0, heads // 2, back)
    for c in range(CHUNKS):
        moving[c] = bwd.z_out(c, moving[c])
    each(heads // 2, heads - heads // 2, back)
    for c in range(CHUNKS):
        moving[c] = bwd.z_back(c, moving[c])
    for c in range(CHUNKS):
        moving[c] = bwd.y_back(c, moving[c])
    for c in range(CHUNKS):
        for copy in moving[c]:
            copy.wait_recv()

        later_bf[pl.ds(c * rows, rows), :] = bwd.b4[c].reshape(rows, HD).astype(BF16)

    fwd.finish()
    for copy in head_copies:
        copy.wait_send()
    bwd.finish()


def finish_kernel(heads, normed, qgrad, kpart, vpart, later_bf, k, v, normed_hbm, qgrad_hbm, kgrad_hbm, vgrad_hbm,
                  kgrad, vgrad, out_sem):
    scale = HD ** (-0.5)
    per = heads // LAST
    outs = []

    def put(src, dst):
        copy = pltpu.make_async_copy(src, dst, out_sem.at[len(outs)])
        copy.start()
        outs.append(copy)

    put(normed, normed_hbm)
    put(qgrad, qgrad_hbm)

    def last(h):
        here = later_bf[sub(h), :]
        kgrad[:, lanes(h)] = (scale * (kpart[:, lanes(h)] + dot_nt(v[:, lanes(h)], here))).astype(BF16)
        vgrad[:, lanes(h)] = (vpart[:, lanes(h)] + scale * dot_nn(k[:, lanes(h)], here)).astype(BF16)

    for c in range(LAST):
        each(c * per, per, last)
        cols = pl.ds(c * per * HD, per * HD)
        put(kgrad.at[:, cols], kgrad_hbm.at[:, cols])
        put(vgrad.at[:, cols], vgrad_hbm.at[:, cols])
    for copy in outs:
        copy.wait()


def local(queries, keys, values, norm_gain, out_grad):
    blk, width = queries.shape
    heads = width // HD
    nz = lax.axis_size("seq") // NY
    nh = lax.axis_size("head")
    rows = heads // CHUNKS * HD
    quarter = rows // NY
    piece = quarter // nz
    vmem = pltpu.VMEM

    def scan_refs():
        return [
            vmem((heads * HD, HD), F32),
            vmem((CHUNKS, NY, quarter, HD), F32),
            vmem((CHUNKS, quarter, HD), F32),
            vmem((CHUNKS, nz, piece, HD), F32),
            vmem((CHUNKS, nz, piece, HD), F32),
            vmem((CHUNKS, nz, piece, HD), F32),
            vmem((CHUNKS, NY, quarter, HD), F32),
            vmem((CHUNKS, NY, quarter, HD), F32),
        ]

    def scan_sems():
        y, zz = 2 * CHUNKS * (NY - 1), 2 * CHUNKS * (nz - 1)
        dma = pltpu.SemaphoreType.DMA
        return [dma((y,)), dma((y,)), dma((zz,)), dma((zz,))]

    big_f32, big_bf16 = vmem((blk, width), F32), vmem((blk, width), BF16)
    scratch = [
        big_bf16, vmem((1, width), F32), big_bf16,
        vmem((heads, 3, HALF, HALF), BF16),
        big_f32, big_bf16,
        vmem((heads * HD, HD), BF16),
        vmem((blk, HD), F32), vmem((blk, HD), F32), vmem((blk, HD), F32), vmem((blk, HD), F32),
        vmem((8, HD), F32), vmem((nh, 8, HD), F32),
        *scan_refs(), *scan_refs(), *scan_sems(), *scan_sems(),
        pltpu.SemaphoreType.DMA((2 * CHUNKS + 3,)),
        pltpu.SemaphoreType.DMA((nh - 1,)),
        pltpu.SemaphoreType.DMA((nh - 1,)),
    ]
    out = jax.ShapeDtypeStruct((blk, width), BF16)
    anywhere, in_vmem = pl.BlockSpec(memory_space=pl.ANY), pl.BlockSpec(memory_space=pltpu.VMEM)
    parts = pl.pallas_call(
        functools.partial(kernel, nz, nh, heads),
        out_shape=(
            big_bf16, big_bf16, big_f32, big_f32, vmem((heads * HD, HD), BF16), big_bf16, big_bf16,
        ),
        in_specs=[anywhere] * 5,
        out_specs=(in_vmem,) * 7,
        scratch_shapes=scratch,
        compiler_params=pltpu.CompilerParams(
            collective_id=0, has_side_effects=True, vmem_limit_bytes=28 * 1024 * 1024
        ),
        name="linear_attention",
    )(*[
        pltpu.with_memory_space_constraint(a, pltpu.HBM)
        for a in (queries, keys, values, norm_gain.reshape(1, width), out_grad)
    ])
    return pl.pallas_call(
        functools.partial(finish_kernel, heads),
        out_shape=(out,) * 4,
        in_specs=[in_vmem] * 7,
        out_specs=(anywhere,) * 4,
        scratch_shapes=[big_bf16, big_bf16, pltpu.SemaphoreType.DMA((2 + 2 * LAST,))],
        compiler_params=pltpu.CompilerParams(vmem_limit_bytes=28 * 1024 * 1024),
        name="key_value_grads",
    )(*parts)


def solution(mesh):
    placed = (P("seq", "head"), P("seq", "head"), P("seq", "head"), P("head"), P("seq", "head"))
    return jax.shard_map(
        local,
        mesh=mesh,
        in_specs=placed,
        out_specs=(P("seq", "head"), P("seq", "head"), P("seq", "head"), P("seq", "head")),
        check_vma=False,
    )
```

```python
import functools

import jax
import jax.numpy as jnp
from jax import lax
from jax.experimental import pallas as pl
from jax.experimental.pallas import tpu as pltpu
from jax.sharding import PartitionSpec as P

HD = 128
BLK = 512
NY = 4
CHUNKS = 4
AHEAD = (3, 3)
BEHIND = (2, 2, 2)
HALF = BLK // 2
F32 = jnp.float32
BF16 = jnp.bfloat16
MESH = pl.DeviceIdType.MESH


def dot_nn(a, b):
    return lax.dot_general(a, b, (((1,), (0,)), ((), ())), preferred_element_type=F32)


def dot_nt(a, b):
    return lax.dot_general(a, b, (((1,), (1,)), ((), ())), preferred_element_type=F32)


def dot_tn(a, b):
    return lax.dot_general(a, b, (((0,), (0,)), ((), ())), preferred_element_type=F32)


def split(a, count):
    parts = []
    for _ in range(count):
        parts.append(a.astype(BF16))
        a = a - parts[-1].astype(F32)
    return parts


class Scan:
    def __init__(self, nz, rows, reverse, refs, sems):
        self.nz, self.rows, self.reverse = nz, rows, reverse
        self.block, self.b1, self.tot, self.b2, self.pre, self.b3, self.ret, self.b4 = refs
        self.ysend, self.yrecv, self.zsend, self.zrecv = sems
        seq = lax.axis_index("seq")
        self.head = lax.axis_index("head")
        self.z, self.y = lax.div(seq, NY), lax.rem(seq, NY)
        self.quarter = rows // NY
        self.piece = self.quarter // nz
        self.sends = []

    def y_copy(self, phase, c, d, src, dst):
        k = (phase * CHUNKS + c) * (NY - 1) + d - 1
        to = self.z * NY + lax.rem(self.y + d, NY)
        return pltpu.make_async_remote_copy(
            src_ref=src, dst_ref=dst, send_sem=self.ysend.at[k], recv_sem=self.yrecv.at[k],
            device_id=(to, self.head), device_id_type=MESH,
        )

    def z_copy(self, phase, c, d, src, dst):
        k = (phase * CHUNKS + c) * (self.nz - 1) + d - 1
        to = lax.rem(self.z + d, self.nz) * NY + self.y
        return pltpu.make_async_remote_copy(
            src_ref=src, dst_ref=dst, send_sem=self.zsend.at[k], recv_sem=self.zrecv.at[k],
            device_id=(to, self.head), device_id_type=MESH,
        )

    def begin(self, copies):
        for copy in copies:
            copy.start()
        self.sends += copies
        return copies

    def y_out(self, c):
        base = c * self.rows

        def part(q):
            return self.block.at[pl.ds(pl.multiple_of(base + q * self.quarter, 8), self.quarter)]

        copies = self.begin([
            self.y_copy(0, c, d, part(lax.rem(self.y + d, NY)), self.b1.at[c, self.y]) for d in (2, 1, 3)
        ])
        self.b1[c, self.y] = part(self.y)[...]
        return copies

    def z_out(self, c, arriving):
        for copy in arriving:
            copy.wait_recv()
        self.tot[c] = (self.b1[c, 0] + self.b1[c, 1]) + (self.b1[c, 2] + self.b1[c, 3])

        def part(j):
            return self.tot.at[c, pl.ds(pl.multiple_of(j * self.piece, 8), self.piece)]

        far = sorted(range(1, self.nz), key=lambda d: -min(d, self.nz - d))
        copies = self.begin([
            self.z_copy(0, c, d, part(lax.rem(self.z + d, self.nz)), self.b2.at[c, self.z]) for d in far
        ])
        self.b2[c, self.z] = part(self.z)[...]
        return copies

    def z_back(self, c, arriving):
        for copy in arriving:
            copy.wait_recv()
        order = range(self.nz)
        total = jnp.zeros((self.piece, HD), F32)
        for j in reversed(order) if self.reverse else order:
            self.pre[c, j] = total
            total = total + self.b2[c, j]
        far = sorted(range(1, self.nz), key=lambda d: -min(d, self.nz - d))
        copies = self.begin([
            self.z_copy(1, c, d, self.pre.at[c, lax.rem(self.z + d, self.nz)], self.b3.at[c, self.z]) for d in far
        ])
        self.b3[c, self.z] = self.pre[c, self.z]
        return copies

    def y_back(self, c, arriving):
        for copy in arriving:
            copy.wait_recv()
        total = self.b3[c].reshape(self.quarter, HD)
        order = range(NY)
        for j in reversed(order) if self.reverse else order:
            self.ret[c, j] = total
            total = total + self.b1[c, j]
        copies = self.begin([
            self.y_copy(1, c, d, self.ret.at[c, lax.rem(self.y + d, NY)], self.b4.at[c, self.y]) for d in (2, 1, 3)
        ])
        self.b4[c, self.y] = self.ret[c, self.y]
        return copies

    def finish(self):
        for copy in self.sends:
            copy.wait_send()


def lanes(h):
    return pl.ds(pl.multiple_of(h * HD, HD), HD)


def sub(h):
    return pl.ds(pl.multiple_of(h * HD, HD), HD)


def each(first, count, body):
    def step(h, _):
        body(h)
        return 0

    lax.fori_loop(first, first + count, step, 0)


def kernel(nz, nh, heads, q_hbm, k_hbm, v_hbm, gain_hbm, g_hbm, normed, qgrad, kgrad, vgrad, kpart_end, vpart_end,
           later_end, k_end, v_end, q, k, v, gain, g, grad_norm, scores, att, dout, kpart, vpart, state_bf, squares,
           products, inv_b, coef_b, head_src, head_dst, *rest):
    fwd_refs, bwd_refs = rest[0:8], rest[8:16]
    fwd_sems, bwd_sems = rest[16:20], rest[20:24]
    in_sem, head_send, head_recv = rest[24:27]
    scale = HD ** (-0.5)
    per = heads // CHUNKS
    rows = per * HD
    width = heads * HD
    seq, head = lax.axis_index("seq"), lax.axis_index("head")
    z, y = lax.div(seq, NY), lax.rem(seq, NY)

    loads = []
    for c in range(CHUNKS):
        cols = pl.ds(c * rows, rows)
        pair = []
        for i, (src, dst) in enumerate(((k_hbm, k), (v_hbm, v))):
            copy = pltpu.make_async_copy(src.at[:, cols], dst.at[:, cols], in_sem.at[2 * c + i])
            copy.start()
            pair.append(copy)
        loads.append(pair)
    late = []
    for i, (src, dst) in enumerate(((q_hbm, q), (g_hbm, g), (gain_hbm, gain))):
        copy = pltpu.make_async_copy(src, dst, in_sem.at[2 * CHUNKS + i])
        copy.start()
        late.append(copy)

    barrier = pltpu.get_barrier_semaphore()
    for d in range(1, NY):
        to = z * NY + lax.rem(y + d, NY)
        pl.semaphore_signal(barrier, inc=1, device_id=(to, head), device_id_type=MESH)
    for d in range(1, nz):
        to = lax.rem(z + d, nz) * NY + y
        pl.semaphore_signal(barrier, inc=1, device_id=(to, head), device_id_type=MESH)
    for d in range(1, nh):
        pl.semaphore_signal(barrier, inc=1, device_id=(seq, lax.rem(head + d, nh)), device_id_type=MESH)

    fwd = Scan(nz, rows, False, fwd_refs, fwd_sems)
    bwd = Scan(nz, rows, True, bwd_refs, bwd_sems)

    def kv(h):
        fwd.block[sub(h), :] = dot_tn(k[:, lanes(h)], v[:, lanes(h)])

    moving = []
    for c in range(CHUNKS):
        for copy in loads[c]:
            copy.wait()
        for h in range(c * per, (c + 1) * per):
            kv(h)
        if c == 0:
            pl.semaphore_wait(barrier, (NY - 1) + (nz - 1) + (nh - 1))
        moving.append(fwd.y_out(c))
    for copy in late:
        copy.wait()

    causal = lax.broadcasted_iota(jnp.int32, (HALF, HALF), 0) >= lax.broadcasted_iota(jnp.int32, (HALF, HALF), 1)

    def tiles(a, b, factor):
        top = jnp.where(causal, dot_nt(a[:HALF], b[:HALF]) * factor, 0.0).astype(BF16)
        low = (dot_nt(a[HALF:], b[:HALF]) * factor).astype(BF16)
        end = jnp.where(causal, dot_nt(a[HALF:], b[HALF:]) * factor, 0.0).astype(BF16)
        return top, low, end

    def intra(h):
        vh = v[:, lanes(h)]
        top, low, end = tiles(q[:, lanes(h)], k[:, lanes(h)], scale)
        scores[h, 0], scores[h, 1], scores[h, 2] = top, low, end
        att[:HALF, lanes(h)] = dot_nn(top, vh[:HALF])
        att[HALF:, lanes(h)] = dot_nn(low, vh[:HALF]) + dot_nn(end, vh[HALF:])
        grad_norm[:, lanes(h)] = g[:, lanes(h)].astype(F32) * gain[:, lanes(h)]

    each(0, AHEAD[0], intra)
    for c in range(CHUNKS):
        moving[c] = fwd.z_out(c, moving[c])
    each(AHEAD[0], AHEAD[1], intra)
    for c in range(CHUNKS):
        moving[c] = fwd.z_back(c, moving[c])
    each(AHEAD[0] + AHEAD[1], heads - AHEAD[0] - AHEAD[1], intra)
    for c in range(CHUNKS):
        moving[c] = fwd.y_back(c, moving[c])
    for c in range(CHUNKS):
        for copy in moving[c]:
            copy.wait_recv()
        here = fwd.b4[c].reshape(rows, HD).astype(BF16)
        state_bf[pl.ds(c * rows, rows), :] = here
        sq, pr = (squares[...], products[...]) if c > 0 else (0.0, 0.0)
        for i in range(per):
            h = c * per + i
            a = att[:, lanes(h)] + scale * dot_nn(q[:, lanes(h)], here[i * HD : (i + 1) * HD])
            att[:, lanes(h)] = a
            sq = sq + a * a
            pr = pr + a * grad_norm[:, lanes(h)]
        squares[...], products[...] = sq, pr

    row = lax.broadcasted_iota(jnp.int32, (8, HD), 0)
    groups = BLK // HD
    packed = jnp.zeros((8, HD), F32)
    for t in range(groups):
        part = pl.ds(t * HD, HD)
        for first, totals in ((0, squares), (groups, products)):
            pick = (row == first + t).astype(BF16)
            packed = packed + dot_nt(
                jnp.concatenate([pick, pick], axis=1), jnp.concatenate(split(totals[part, :], 2), axis=1)
            )
    head_src[...] = packed
    head_copies = []
    for d in range(1, nh):
        copy = pltpu.make_async_remote_copy(
            src_ref=head_src, dst_ref=head_dst.at[head], send_sem=head_send.at[d - 1], recv_sem=head_recv.at[d - 1],
            device_id=(seq, lax.rem(head + d, nh)), device_id_type=MESH,
        )
        copy.start()
        head_copies.append(copy)
    head_dst[head] = packed
    for copy in head_copies:
        copy.wait_recv()
    sums = head_dst[0]
    for j in range(1, nh):
        sums = sums + head_dst[j]
    full = nh * width
    inv = 1.0 / jnp.sqrt(sums[:groups] / full + 1e-06)
    proj = (sums[groups:] * inv) / full
    both = jnp.concatenate(split(jnp.concatenate([inv, (inv * proj) * inv], axis=0), 3), axis=0)
    for t in range(groups):
        part = pl.ds(t * HD, HD)
        for first, spread in ((0, inv_b), (groups, coef_b)):
            pick = (row == first + t).astype(BF16)
            spread[part, :] = dot_tn(both, jnp.concatenate([pick, pick, pick], axis=0))

    def grad(h):
        d = (grad_norm[:, lanes(h)] * inv_b[...] - att[:, lanes(h)] * coef_b[...]).astype(BF16)
        dout[:, lanes(h)] = d
        bwd.block[sub(h), :] = dot_tn(q[:, lanes(h)], d)

    for c in range(CHUNKS):
        for h in range(c * per, (c + 1) * per):
            grad(h)
        moving[c] = bwd.y_out(c)

    def back(h):
        qh, kh, vh, d = q[:, lanes(h)], k[:, lanes(h)], v[:, lanes(h)], dout[:, lanes(h)]
        normed[:, lanes(h)] = (att[:, lanes(h)] * inv_b[...] * gain[:, lanes(h)]).astype(BF16)
        top, low, end = tiles(d, vh, 1.0)
        carried = dot_nt(d, state_bf[sub(h), :])
        qgrad[:HALF, lanes(h)] = (scale * (dot_nn(top, kh[:HALF]) + carried[:HALF])).astype(BF16)
        qgrad[HALF:, lanes(h)] = (
            scale * (dot_nn(low, kh[:HALF]) + dot_nn(end, kh[HALF:]) + carried[HALF:])
        ).astype(BF16)
        kpart[:HALF, lanes(h)] = dot_tn(top, qh[:HALF]) + dot_tn(low, qh[HALF:])
        kpart[HALF:, lanes(h)] = dot_tn(end, qh[HALF:])
        vpart[:HALF, lanes(h)] = dot_tn(scores[h, 0], d[:HALF]) + dot_tn(scores[h, 1], d[HALF:])
        vpart[HALF:, lanes(h)] = dot_tn(scores[h, 2], d[HALF:])

    done = 0
    each(done, BEHIND[0], back)
    done += BEHIND[0]
    for c in range(CHUNKS):
        moving[c] = bwd.z_out(c, moving[c])
    each(done, BEHIND[1], back)
    done += BEHIND[1]
    for c in range(CHUNKS):
        moving[c] = bwd.z_back(c, moving[c])
    each(done, BEHIND[2], back)
    done += BEHIND[2]
    for c in range(CHUNKS):
        moving[c] = bwd.y_back(c, moving[c])
    each(done, heads - done, back)
    end = pl.ds((CHUNKS - 1) * rows, rows)
    k_end[...], v_end[...] = k[:, end], v[:, end]
    kpart_end[...], vpart_end[...] = kpart[:, end], vpart[:, end]
    for c in range(CHUNKS):
        for copy in moving[c]:
            copy.wait_recv()
        here = bwd.b4[c].reshape(rows, HD).astype(BF16)
        if c == CHUNKS - 1:
            later_end[...] = here
            break
        for i in range(per):
            h = c * per + i
            one = here[i * HD : (i + 1) * HD]
            kgrad[:, lanes(h)] = (scale * (kpart[:, lanes(h)] + dot_nt(v[:, lanes(h)], one))).astype(BF16)
            vgrad[:, lanes(h)] = (vpart[:, lanes(h)] + scale * dot_nn(k[:, lanes(h)], one)).astype(BF16)

    fwd.finish()
    for copy in head_copies:
        copy.wait_send()
    bwd.finish()


def finish_kernel(per, normed, qgrad, kgrad, vgrad, kpart, vpart, later, k, v, normed_hbm, qgrad_hbm, kgrad_hbm,
                  vgrad_hbm, kgrad_end, vgrad_end, out_sem):
    scale = HD ** (-0.5)
    outs = []

    def put(src, dst):
        copy = pltpu.make_async_copy(src, dst, out_sem.at[len(outs)])
        copy.start()
        outs.append(copy)

    begun = kgrad.shape[1] - per * HD
    for src, dst in ((kgrad, kgrad_hbm), (vgrad, vgrad_hbm)):
        put(src.at[:, pl.ds(0, begun)], dst.at[:, pl.ds(0, begun)])
    put(normed, normed_hbm)
    put(qgrad, qgrad_hbm)
    for h in range(per):
        kgrad_end[:, lanes(h)] = (scale * (kpart[:, lanes(h)] + dot_nt(v[:, lanes(h)], later[sub(h), :]))).astype(BF16)
        vgrad_end[:, lanes(h)] = (vpart[:, lanes(h)] + scale * dot_nn(k[:, lanes(h)], later[sub(h), :])).astype(BF16)
    for src, dst in ((kgrad_end, kgrad_hbm), (vgrad_end, vgrad_hbm)):
        put(src, dst.at[:, pl.ds(begun, per * HD)])
    for copy in outs:
        copy.wait()


def local(queries, keys, values, norm_gain, out_grad):
    blk, width = queries.shape
    heads = width // HD
    nz = lax.axis_size("seq") // NY
    nh = lax.axis_size("head")
    rows = heads // CHUNKS * HD
    quarter = rows // NY
    piece = quarter // nz
    vmem = pltpu.VMEM

    def scan_refs():
        return [
            vmem((heads * HD, HD), F32),
            vmem((CHUNKS, NY, quarter, HD), F32),
            vmem((CHUNKS, quarter, HD), F32),
            vmem((CHUNKS, nz, piece, HD), F32),
            vmem((CHUNKS, nz, piece, HD), F32),
            vmem((CHUNKS, nz, piece, HD), F32),
            vmem((CHUNKS, NY, quarter, HD), F32),
            vmem((CHUNKS, NY, quarter, HD), F32),
        ]

    def scan_sems():
        y, zz = 2 * CHUNKS * (NY - 1), 2 * CHUNKS * (nz - 1)
        dma = pltpu.SemaphoreType.DMA
        return [dma((y,)), dma((y,)), dma((zz,)), dma((zz,))]

    big_f32, big_bf16 = vmem((blk, width), F32), vmem((blk, width), BF16)
    end_f32, end_bf16 = vmem((blk, rows), F32), vmem((blk, rows), BF16)
    scratch = [
        big_bf16, big_bf16, big_bf16, vmem((1, width), F32), big_bf16, big_f32,
        vmem((heads, 3, HALF, HALF), BF16),
        big_f32, big_bf16, big_f32, big_f32,
        vmem((heads * HD, HD), BF16),
        vmem((blk, HD), F32), vmem((blk, HD), F32), vmem((blk, HD), F32), vmem((blk, HD), F32),
        vmem((8, HD), F32), vmem((nh, 8, HD), F32),
        *scan_refs(), *scan_refs(), *scan_sems(), *scan_sems(),
        pltpu.SemaphoreType.DMA((2 * CHUNKS + 3,)),
        pltpu.SemaphoreType.DMA((nh - 1,)),
        pltpu.SemaphoreType.DMA((nh - 1,)),
    ]
    out = jax.ShapeDtypeStruct((blk, width), BF16)
    anywhere, in_vmem = pl.BlockSpec(memory_space=pl.ANY), pl.BlockSpec(memory_space=pltpu.VMEM)
    parts = pl.pallas_call(
        functools.partial(kernel, nz, nh, heads),
        out_shape=(
            big_bf16, big_bf16, big_bf16, big_bf16, end_f32, end_f32, vmem((rows, HD), BF16), end_bf16, end_bf16,
        ),
        in_specs=[anywhere] * 5,
        out_specs=(in_vmem,) * 9,
        scratch_shapes=scratch,
        compiler_params=pltpu.CompilerParams(
            collective_id=0, has_side_effects=True, vmem_limit_bytes=40 * 1024 * 1024
        ),
        name="linear_attention",
    )(*[
        pltpu.with_memory_space_constraint(a, pltpu.HBM)
        for a in (queries, keys, values, norm_gain.reshape(1, width), out_grad)
    ])
    return pl.pallas_call(
        functools.partial(finish_kernel, heads // CHUNKS),
        out_shape=(out,) * 4,
        in_specs=[in_vmem] * 9,
        out_specs=(anywhere,) * 4,
        scratch_shapes=[end_bf16, end_bf16, pltpu.SemaphoreType.DMA((6,))],
        compiler_params=pltpu.CompilerParams(vmem_limit_bytes=28 * 1024 * 1024),
        name="key_value_grads",
    )(*parts)


def solution(mesh):
    placed = (P("seq", "head"), P("seq", "head"), P("seq", "head"), P("head"), P("seq", "head"))
    return jax.shard_map(
        local,
        mesh=mesh,
        in_specs=placed,
        out_specs=(P("seq", "head"), P("seq", "head"), P("seq", "head"), P("seq", "head")),
        check_vma=False,
    )
```

```python
import functools

import jax
import jax.numpy as jnp
from jax import lax
from jax.experimental import pallas as pl
from jax.experimental.pallas import tpu as pltpu
from jax.sharding import PartitionSpec as P

HD = 128
BLK = 512
NY = 4
CHUNKS = 4
ORDER = (1, 2, 0, 3)
ARRIVAL = (1, 2, 0, 3)
AHEAD = (3, 3)
BEHIND = (2, 2, 2)
HALF = BLK // 2
F32 = jnp.float32
BF16 = jnp.bfloat16
MESH = pl.DeviceIdType.MESH


def dot_nn(a, b):
    return lax.dot_general(a, b, (((1,), (0,)), ((), ())), preferred_element_type=F32)


def dot_nt(a, b):
    return lax.dot_general(a, b, (((1,), (1,)), ((), ())), preferred_element_type=F32)


def dot_tn(a, b):
    return lax.dot_general(a, b, (((0,), (0,)), ((), ())), preferred_element_type=F32)


def split(a, count):
    parts = []
    for _ in range(count):
        parts.append(a.astype(BF16))
        a = a - parts[-1].astype(F32)
    return parts


def far_first(count):
    return sorted(range(1, count), key=lambda d: -min(d, count - d))


class Scan:
    def __init__(self, nz, rows, reverse, refs, sems):
        self.nz, self.rows, self.reverse = nz, rows, reverse
        self.block, self.b1, self.tot, self.b2, self.pre, self.b3, self.ret, self.b4 = refs[:8]
        self.a1, self.a2, self.a3, self.a4, self.a5 = refs[8:]
        self.ysend, self.yrecv, self.zsend, self.zrecv = sems
        seq = lax.axis_index("seq")
        self.head = lax.axis_index("head")
        self.z, self.y = lax.div(seq, NY), lax.rem(seq, NY)
        self.quarter = rows // NY
        self.piece = self.quarter // nz
        self.sends = []

    def y_copy(self, phase, c, d, src, dst):
        k = (phase * CHUNKS + c) * (NY - 1) + d - 1
        to = self.z * NY + lax.rem(self.y + d, NY)
        return pltpu.make_async_remote_copy(
            src_ref=src, dst_ref=dst, send_sem=self.ysend.at[k], recv_sem=self.yrecv.at[k],
            device_id=(to, self.head), device_id_type=MESH,
        )

    def z_copy(self, phase, c, d, src, dst):
        k = (phase * CHUNKS + c) * (self.nz - 1) + d - 1
        to = lax.rem(self.z + d, self.nz) * NY + self.y
        return pltpu.make_async_remote_copy(
            src_ref=src, dst_ref=dst, send_sem=self.zsend.at[k], recv_sem=self.zrecv.at[k],
            device_id=(to, self.head), device_id_type=MESH,
        )

    def begin(self, copies):
        for copy in copies:
            copy.start()
        self.sends += copies
        return copies

    def y_out(self, c):
        base = c * self.rows

        def part(q):
            return self.block.at[pl.ds(pl.multiple_of(base + q * self.quarter, 8), self.quarter)]

        copies = self.begin([
            self.y_copy(0, c, d, part(lax.rem(self.y + d, NY)), self.b1.at[c, self.y]) for d in (2, 1, 3)
        ])
        self.b1[c, self.y] = part(self.y)[...]
        return copies

    def z_out(self, c, arriving):
        for copy in arriving:
            copy.wait_recv()
        self.tot[c] = (self.b1[c, 0] + self.b1[c, 1]) + (self.b1[c, 2] + self.b1[c, 3])

        def part(j):
            return self.tot.at[c, pl.ds(pl.multiple_of(j * self.piece, 8), self.piece)]

        copies = self.begin([
            self.z_copy(0, c, d, part(lax.rem(self.z + d, self.nz)), self.b2.at[c, self.z]) for d in far_first(self.nz)
        ])
        self.b2[c, self.z] = part(self.z)[...]
        return copies

    def z_back(self, c, arriving):
        for copy in arriving:
            copy.wait_recv()
        order = range(self.nz)
        total = jnp.zeros((self.piece, HD), F32)
        for j in reversed(order) if self.reverse else order:
            self.pre[c, j] = total
            total = total + self.b2[c, j]
        copies = self.begin([
            self.z_copy(1, c, d, self.pre.at[c, lax.rem(self.z + d, self.nz)], self.b3.at[c, self.z]) for d in far_first(self.nz)
        ])
        self.b3[c, self.z] = self.pre[c, self.z]
        return copies

    def y_back(self, c, arriving):
        for copy in arriving:
            copy.wait_recv()
        total = self.b3[c].reshape(self.quarter, HD)
        order = range(NY)
        for j in reversed(order) if self.reverse else order:
            self.ret[c, j] = total
            total = total + self.b1[c, j]
        copies = self.begin([
            self.y_copy(1, c, d, self.ret.at[c, lax.rem(self.y + d, NY)], self.b4.at[c, self.y]) for d in (2, 1, 3)
        ])
        self.b4[c, self.y] = self.ret[c, self.y]
        return copies

    def a_out(self):
        height = self.rows // self.nz

        def part(j):
            return self.block.at[pl.ds(pl.multiple_of(j * height, 8), height)]

        copies = self.begin([
            self.z_copy(0, 0, d, part(lax.rem(self.z + d, self.nz)), self.a1.at[self.z]) for d in far_first(self.nz)
        ])
        self.a1[self.z] = part(self.z)[...]
        return copies

    def a_mid(self, arriving):
        for copy in arriving:
            copy.wait_recv()
        height = self.rows // self.nz // NY

        def part(q):
            return self.a1.at[:, pl.ds(pl.multiple_of(q * height, 8), height)]

        copies = self.begin([
            self.y_copy(0, 0, d, part(lax.rem(self.y + d, NY)), self.a2.at[self.y]) for d in (2, 1, 3)
        ])
        self.a2[self.y] = part(self.y)[...]
        return copies

    def a_back(self, arriving):
        for copy in arriving:
            copy.wait_recv()
        order = [(j, i) for j in range(self.nz) for i in range(NY)]
        total = jnp.zeros(self.a2.shape[2:], F32)
        for j, i in reversed(order) if self.reverse else order:
            self.a3[i, j] = total
            total = total + self.a2[i, j]
        copies = self.begin([
            self.y_copy(1, 0, d, self.a3.at[lax.rem(self.y + d, NY)], self.a4.at[self.y]) for d in (2, 1, 3)
        ])
        self.a4[self.y] = self.a3[self.y]
        return copies

    def a_end(self, arriving):
        for copy in arriving:
            copy.wait_recv()
        copies = self.begin([
            self.z_copy(1, 0, d, self.a4.at[:, lax.rem(self.z + d, self.nz)], self.a5.at[self.z])
            for d in far_first(self.nz)
        ])
        self.a5[self.z] = self.a4[:, self.z]
        return copies

    def first(self, c):
        return self.a_out() if c == 0 else self.y_out(c)

    def second(self, moving):
        for c in ORDER:
            moving[c] = self.a_mid(moving[c]) if c == 0 else self.z_out(c, moving[c])

    def third(self, moving):
        for c in ORDER:
            moving[c] = self.a_back(moving[c]) if c == 0 else self.z_back(c, moving[c])

    def fourth(self, moving):
        for c in ORDER:
            moving[c] = self.a_end(moving[c]) if c == 0 else self.y_back(c, moving[c])

    def result(self, c, arriving):
        for copy in arriving:
            copy.wait_recv()
        return (self.a5[...] if c == 0 else self.b4[c]).reshape(self.rows, HD).astype(BF16)

    def finish(self):
        for copy in self.sends:
            copy.wait_send()


def lanes(h):
    return pl.ds(pl.multiple_of(h * HD, HD), HD)


def sub(h):
    return pl.ds(pl.multiple_of(h * HD, HD), HD)


def each(first, count, body):
    def step(h, _):
        body(h)
        return 0

    lax.fori_loop(first, first + count, step, 0)


def kernel(nz, nh, heads, q_hbm, k_hbm, v_hbm, gain_hbm, g_hbm, normed, qgrad, kgrad, vgrad, kpart_end, vpart_end,
           later_end, k_end, v_end, q, k, v, gain, g, grad_norm, scores, att, dout, kpart, vpart, state_bf, squares,
           products, inv_b, coef_b, head_src, head_dst, *rest):
    fwd_refs, bwd_refs = rest[0:13], rest[13:26]
    fwd_sems, bwd_sems = rest[26:30], rest[30:34]
    in_sem, head_send, head_recv = rest[34:37]
    scale = HD ** (-0.5)
    per = heads // CHUNKS
    rows = per * HD
    width = heads * HD
    seq, head = lax.axis_index("seq"), lax.axis_index("head")
    z, y = lax.div(seq, NY), lax.rem(seq, NY)

    loads = []

    def load(c):
        cols = pl.ds(c * rows, rows)
        pair = []
        for i, (src, dst) in enumerate(((k_hbm, k), (v_hbm, v))):
            copy = pltpu.make_async_copy(src.at[:, cols], dst.at[:, cols], in_sem.at[2 * c + i])
            copy.start()
            pair.append(copy)
        loads.append(pair)

    load(0)
    barrier = pltpu.get_barrier_semaphore()
    for d in far_first(nz):
        to = lax.rem(z + d, nz) * NY + y
        pl.semaphore_signal(barrier, inc=1, device_id=(to, head), device_id_type=MESH)
    for d in range(1, nh):
        pl.semaphore_signal(barrier, inc=1, device_id=(seq, lax.rem(head + d, nh)), device_id_type=MESH)
    for d in far_first(NY):
        to = z * NY + lax.rem(y + d, NY)
        pl.semaphore_signal(barrier, inc=1, device_id=(to, head), device_id_type=MESH)

    for c in range(1, CHUNKS):
        load(c)
    late = []
    for i, (src, dst) in enumerate(((q_hbm, q), (g_hbm, g), (gain_hbm, gain))):
        copy = pltpu.make_async_copy(src, dst, in_sem.at[2 * CHUNKS + i])
        copy.start()
        late.append(copy)

    fwd = Scan(nz, rows, False, fwd_refs, fwd_sems)
    bwd = Scan(nz, rows, True, bwd_refs, bwd_sems)

    def kv(h):
        fwd.block[sub(h), :] = dot_tn(k[:, lanes(h)], v[:, lanes(h)])

    moving = []
    for c in range(CHUNKS):
        for copy in loads[c]:
            copy.wait()
        for h in range(c * per, (c + 1) * per):
            kv(h)
        if c == 0:
            pl.semaphore_wait(barrier, (NY - 1) + (nz - 1) + (nh - 1))
        moving.append(fwd.first(c))
    for copy in late:
        copy.wait()

    causal = lax.broadcasted_iota(jnp.int32, (HALF, HALF), 0) >= lax.broadcasted_iota(jnp.int32, (HALF, HALF), 1)

    def tiles(a, b, factor):
        top = jnp.where(causal, dot_nt(a[:HALF], b[:HALF]) * factor, 0.0).astype(BF16)
        low = (dot_nt(a[HALF:], b[:HALF]) * factor).astype(BF16)
        end = jnp.where(causal, dot_nt(a[HALF:], b[HALF:]) * factor, 0.0).astype(BF16)
        return top, low, end

    def intra(h):
        vh = v[:, lanes(h)]
        top, low, end = tiles(q[:, lanes(h)], k[:, lanes(h)], scale)
        scores[h, 0], scores[h, 1], scores[h, 2] = top, low, end
        att[:HALF, lanes(h)] = dot_nn(top, vh[:HALF])
        att[HALF:, lanes(h)] = dot_nn(low, vh[:HALF]) + dot_nn(end, vh[HALF:])
        grad_norm[:, lanes(h)] = g[:, lanes(h)].astype(F32) * gain[:, lanes(h)]

    each(0, AHEAD[0], intra)
    fwd.second(moving)
    each(AHEAD[0], AHEAD[1], intra)
    fwd.third(moving)
    each(AHEAD[0] + AHEAD[1], heads - AHEAD[0] - AHEAD[1], intra)
    fwd.fourth(moving)
    for c in ARRIVAL:
        here = fwd.result(c, moving[c])
        state_bf[pl.ds(c * rows, rows), :] = here
        sq, pr = (0.0, 0.0) if c == ARRIVAL[0] else (squares[...], products[...])
        for i in range(per):
            h = c * per + i
            a = att[:, lanes(h)] + scale * dot_nn(q[:, lanes(h)], here[i * HD : (i + 1) * HD])
            att[:, lanes(h)] = a
            sq = sq + a * a
            pr = pr + a * grad_norm[:, lanes(h)]
        squares[...], products[...] = sq, pr

    row = lax.broadcasted_iota(jnp.int32, (8, HD), 0)
    groups = BLK // HD
    packed = jnp.zeros((8, HD), F32)
    for t in range(groups):
        part = pl.ds(t * HD, HD)
        for first, totals in ((0, squares), (groups, products)):
            pick = (row == first + t).astype(BF16)
            packed = packed + dot_nt(
                jnp.concatenate([pick, pick], axis=1), jnp.concatenate(split(totals[part, :], 2), axis=1)
            )
    head_src[...] = packed
    head_copies = []
    for d in range(1, nh):
        copy = pltpu.make_async_remote_copy(
            src_ref=head_src, dst_ref=head_dst.at[head], send_sem=head_send.at[d - 1], recv_sem=head_recv.at[d - 1],
            device_id=(seq, lax.rem(head + d, nh)), device_id_type=MESH,
        )
        copy.start()
        head_copies.append(copy)
    head_dst[head] = packed
    for copy in head_copies:
        copy.wait_recv()
    sums = head_dst[0]
    for j in range(1, nh):
        sums = sums + head_dst[j]
    full = nh * width
    inv = 1.0 / jnp.sqrt(sums[:groups] / full + 1e-06)
    proj = (sums[groups:] * inv) / full
    both = jnp.concatenate(split(jnp.concatenate([inv, (inv * proj) * inv], axis=0), 3), axis=0)
    for t in range(groups):
        part = pl.ds(t * HD, HD)
        for first, spread in ((0, inv_b), (groups, coef_b)):
            pick = (row == first + t).astype(BF16)
            spread[part, :] = dot_tn(both, jnp.concatenate([pick, pick, pick], axis=0))

    def grad(h):
        d = (grad_norm[:, lanes(h)] * inv_b[...] - att[:, lanes(h)] * coef_b[...]).astype(BF16)
        dout[:, lanes(h)] = d
        bwd.block[sub(h), :] = dot_tn(q[:, lanes(h)], d)

    for c in range(CHUNKS):
        for h in range(c * per, (c + 1) * per):
            grad(h)
        moving[c] = bwd.first(c)

    def back(h):
        qh, kh, vh, d = q[:, lanes(h)], k[:, lanes(h)], v[:, lanes(h)], dout[:, lanes(h)]
        normed[:, lanes(h)] = (att[:, lanes(h)] * inv_b[...] * gain[:, lanes(h)]).astype(BF16)
        top, low, end = tiles(d, vh, 1.0)
        carried = dot_nt(d, state_bf[sub(h), :])
        qgrad[:HALF, lanes(h)] = (scale * (dot_nn(top, kh[:HALF]) + carried[:HALF])).astype(BF16)
        qgrad[HALF:, lanes(h)] = (
            scale * (dot_nn(low, kh[:HALF]) + dot_nn(end, kh[HALF:]) + carried[HALF:])
        ).astype(BF16)
        kpart[:HALF, lanes(h)] = dot_tn(top, qh[:HALF]) + dot_tn(low, qh[HALF:])
        kpart[HALF:, lanes(h)] = dot_tn(end, qh[HALF:])
        vpart[:HALF, lanes(h)] = dot_tn(scores[h, 0], d[:HALF]) + dot_tn(scores[h, 1], d[HALF:])
        vpart[HALF:, lanes(h)] = dot_tn(scores[h, 2], d[HALF:])

    done = 0
    each(done, BEHIND[0], back)
    done += BEHIND[0]
    bwd.second(moving)
    each(done, BEHIND[1], back)
    done += BEHIND[1]
    bwd.third(moving)
    each(done, BEHIND[2], back)
    done += BEHIND[2]
    bwd.fourth(moving)
    each(done, heads - done, back)
    end = pl.ds((CHUNKS - 1) * rows, rows)
    k_end[...], v_end[...] = k[:, end], v[:, end]
    kpart_end[...], vpart_end[...] = kpart[:, end], vpart[:, end]
    for c in ARRIVAL:
        here = bwd.result(c, moving[c])
        if c == CHUNKS - 1:
            later_end[...] = here
            break
        for i in range(per):
            h = c * per + i
            one = here[i * HD : (i + 1) * HD]
            kgrad[:, lanes(h)] = (scale * (kpart[:, lanes(h)] + dot_nt(v[:, lanes(h)], one))).astype(BF16)
            vgrad[:, lanes(h)] = (vpart[:, lanes(h)] + scale * dot_nn(k[:, lanes(h)], one)).astype(BF16)

    fwd.finish()
    for copy in head_copies:
        copy.wait_send()
    bwd.finish()


def finish_kernel(per, normed, qgrad, kgrad, vgrad, kpart, vpart, later, k, v, normed_hbm, qgrad_hbm, kgrad_hbm,
                  vgrad_hbm, kgrad_end, vgrad_end, out_sem):
    scale = HD ** (-0.5)
    outs = []

    def put(src, dst):
        copy = pltpu.make_async_copy(src, dst, out_sem.at[len(outs)])
        copy.start()
        outs.append(copy)

    begun = kgrad.shape[1] - per * HD
    for src, dst in ((kgrad, kgrad_hbm), (vgrad, vgrad_hbm)):
        put(src.at[:, pl.ds(0, begun)], dst.at[:, pl.ds(0, begun)])
    put(normed, normed_hbm)
    put(qgrad, qgrad_hbm)
    for h in range(per):
        kgrad_end[:, lanes(h)] = (scale * (kpart[:, lanes(h)] + dot_nt(v[:, lanes(h)], later[sub(h), :]))).astype(BF16)
        vgrad_end[:, lanes(h)] = (vpart[:, lanes(h)] + scale * dot_nn(k[:, lanes(h)], later[sub(h), :])).astype(BF16)
    for src, dst in ((kgrad_end, kgrad_hbm), (vgrad_end, vgrad_hbm)):
        put(src, dst.at[:, pl.ds(begun, per * HD)])
    for copy in outs:
        copy.wait()


def local(queries, keys, values, norm_gain, out_grad):
    blk, width = queries.shape
    heads = width // HD
    nz = lax.axis_size("seq") // NY
    nh = lax.axis_size("head")
    rows = heads // CHUNKS * HD
    quarter = rows // NY
    piece = quarter // nz
    vmem = pltpu.VMEM

    def scan_refs():
        return [
            vmem((heads * HD, HD), F32),
            vmem((CHUNKS, NY, quarter, HD), F32),
            vmem((CHUNKS, quarter, HD), F32),
            vmem((CHUNKS, nz, piece, HD), F32),
            vmem((CHUNKS, nz, piece, HD), F32),
            vmem((CHUNKS, nz, piece, HD), F32),
            vmem((CHUNKS, NY, quarter, HD), F32),
            vmem((CHUNKS, NY, quarter, HD), F32),
            vmem((nz, rows // nz, HD), F32),
            vmem((NY, nz, rows // nz // NY, HD), F32),
            vmem((NY, nz, rows // nz // NY, HD), F32),
            vmem((NY, nz, rows // nz // NY, HD), F32),
            vmem((nz, NY, rows // nz // NY, HD), F32),
        ]

    def scan_sems():
        y, zz = 2 * CHUNKS * (NY - 1), 2 * CHUNKS * (nz - 1)
        dma = pltpu.SemaphoreType.DMA
        return [dma((y,)), dma((y,)), dma((zz,)), dma((zz,))]

    big_f32, big_bf16 = vmem((blk, width), F32), vmem((blk, width), BF16)
    end_f32, end_bf16 = vmem((blk, rows), F32), vmem((blk, rows), BF16)
    scratch = [
        big_bf16, big_bf16, big_bf16, vmem((1, width), F32), big_bf16, big_f32,
        vmem((heads, 3, HALF, HALF), BF16),
        big_f32, big_bf16, big_f32, big_f32,
        vmem((heads * HD, HD), BF16),
        vmem((blk, HD), F32), vmem((blk, HD), F32), vmem((blk, HD), F32), vmem((blk, HD), F32),
        vmem((8, HD), F32), vmem((nh, 8, HD), F32),
        *scan_refs(), *scan_refs(), *scan_sems(), *scan_sems(),
        pltpu.SemaphoreType.DMA((2 * CHUNKS + 3,)),
        pltpu.SemaphoreType.DMA((nh - 1,)),
        pltpu.SemaphoreType.DMA((nh - 1,)),
    ]
    out = jax.ShapeDtypeStruct((blk, width), BF16)
    anywhere, in_vmem = pl.BlockSpec(memory_space=pl.ANY), pl.BlockSpec(memory_space=pltpu.VMEM)
    parts = pl.pallas_call(
        functools.partial(kernel, nz, nh, heads),
        out_shape=(
            big_bf16, big_bf16, big_bf16, big_bf16, end_f32, end_f32, vmem((rows, HD), BF16), end_bf16, end_bf16,
        ),
        in_specs=[anywhere] * 5,
        out_specs=(in_vmem,) * 9,
        scratch_shapes=scratch,
        compiler_params=pltpu.CompilerParams(
            collective_id=0, has_side_effects=True, vmem_limit_bytes=40 * 1024 * 1024
        ),
        name="linear_attention",
    )(*[
        pltpu.with_memory_space_constraint(a, pltpu.HBM)
        for a in (queries, keys, values, norm_gain.reshape(1, width), out_grad)
    ])
    return pl.pallas_call(
        functools.partial(finish_kernel, heads // CHUNKS),
        out_shape=(out,) * 4,
        in_specs=[in_vmem] * 9,
        out_specs=(anywhere,) * 4,
        scratch_shapes=[end_bf16, end_bf16, pltpu.SemaphoreType.DMA((6,))],
        compiler_params=pltpu.CompilerParams(vmem_limit_bytes=28 * 1024 * 1024),
        name="key_value_grads",
    )(*parts)


def solution(mesh):
    placed = (P("seq", "head"), P("seq", "head"), P("seq", "head"), P("head"), P("seq", "head"))
    return jax.shard_map(
        local,
        mesh=mesh,
        in_specs=placed,
        out_specs=(P("seq", "head"), P("seq", "head"), P("seq", "head"), P("seq", "head")),
        check_vma=False,
    )
```

```python
import functools

import jax
import jax.numpy as jnp
from jax import lax
from jax.experimental import pallas as pl
from jax.experimental.pallas import tpu as pltpu
from jax.sharding import PartitionSpec as P

HD = 128
BLK = 512
NY = 4
CHUNKS = 4
ORDER = (1, 2, 0, 3)
ARRIVAL = (1, 2, 0, 3)
AHEAD = (3, 3)
BEHIND = (2, 2, 2)
HALF = BLK // 2
F32 = jnp.float32
BF16 = jnp.bfloat16
MESH = pl.DeviceIdType.MESH


def dot_nn(a, b):
    return lax.dot_general(a, b, (((1,), (0,)), ((), ())), preferred_element_type=F32)


def dot_nt(a, b):
    return lax.dot_general(a, b, (((1,), (1,)), ((), ())), preferred_element_type=F32)


def dot_tn(a, b):
    return lax.dot_general(a, b, (((0,), (0,)), ((), ())), preferred_element_type=F32)


def split(a, count):
    parts = []
    for _ in range(count):
        parts.append(a.astype(BF16))
        a = a - parts[-1].astype(F32)
    return parts


def far_first(count):
    return sorted(range(1, count), key=lambda d: -min(d, count - d))


class Scan:
    def __init__(self, nz, rows, reverse, refs, sems):
        self.nz, self.rows, self.reverse = nz, rows, reverse
        self.block, self.b1, self.tot, self.b2, self.pre, self.b3, self.ret, self.b4 = refs[:8]
        self.a1, self.a2, self.a3, self.a4, self.a5 = refs[8:]
        self.ysend, self.yrecv, self.zsend, self.zrecv = sems
        seq = lax.axis_index("seq")
        self.head = lax.axis_index("head")
        self.z, self.y = lax.div(seq, NY), lax.rem(seq, NY)
        self.quarter = rows // NY
        self.piece = self.quarter // nz
        self.sends = []

    def y_copy(self, phase, c, d, src, dst):
        k = (phase * CHUNKS + c) * (NY - 1) + d - 1
        to = self.z * NY + lax.rem(self.y + d, NY)
        return pltpu.make_async_remote_copy(
            src_ref=src, dst_ref=dst, send_sem=self.ysend.at[k], recv_sem=self.yrecv.at[k],
            device_id=(to, self.head), device_id_type=MESH,
        )

    def z_copy(self, phase, c, d, src, dst):
        k = (phase * CHUNKS + c) * (self.nz - 1) + d - 1
        to = lax.rem(self.z + d, self.nz) * NY + self.y
        return pltpu.make_async_remote_copy(
            src_ref=src, dst_ref=dst, send_sem=self.zsend.at[k], recv_sem=self.zrecv.at[k],
            device_id=(to, self.head), device_id_type=MESH,
        )

    def begin(self, copies):
        for copy in copies:
            copy.start()
        self.sends += copies
        return copies

    def y_out(self, c):
        base = c * self.rows

        def part(q):
            return self.block.at[pl.ds(pl.multiple_of(base + q * self.quarter, 8), self.quarter)]

        copies = self.begin([
            self.y_copy(0, c, d, part(lax.rem(self.y + d, NY)), self.b1.at[c, self.y]) for d in (2, 1, 3)
        ])
        self.b1[c, self.y] = part(self.y)[...]
        return copies

    def z_out(self, c, arriving):
        for copy in arriving:
            copy.wait_recv()
        self.tot[c] = (self.b1[c, 0] + self.b1[c, 1]) + (self.b1[c, 2] + self.b1[c, 3])

        def part(j):
            return self.tot.at[c, pl.ds(pl.multiple_of(j * self.piece, 8), self.piece)]

        copies = self.begin([
            self.z_copy(0, c, d, part(lax.rem(self.z + d, self.nz)), self.b2.at[c, self.z]) for d in far_first(self.nz)
        ])
        self.b2[c, self.z] = part(self.z)[...]
        return copies

    def z_back(self, c, arriving):
        for copy in arriving:
            copy.wait_recv()
        order = range(self.nz)
        total = jnp.zeros((self.piece, HD), F32)
        for j in reversed(order) if self.reverse else order:
            self.pre[c, j] = total
            total = total + self.b2[c, j]
        copies = self.begin([
            self.z_copy(1, c, d, self.pre.at[c, lax.rem(self.z + d, self.nz)], self.b3.at[c, self.z]) for d in far_first(self.nz)
        ])
        self.b3[c, self.z] = self.pre[c, self.z]
        return copies

    def y_back(self, c, arriving):
        for copy in arriving:
            copy.wait_recv()
        total = self.b3[c].reshape(self.quarter, HD)
        order = range(NY)
        for j in reversed(order) if self.reverse else order:
            self.ret[c, j] = total
            total = total + self.b1[c, j]
        copies = self.begin([
            self.y_copy(1, c, d, self.ret.at[c, lax.rem(self.y + d, NY)], self.b4.at[c, self.y]) for d in (2, 1, 3)
        ])
        self.b4[c, self.y] = self.ret[c, self.y]
        return copies

    def a_out(self):
        height = self.rows // self.nz

        def part(j):
            return self.block.at[pl.ds(pl.multiple_of(j * height, 8), height)]

        copies = self.begin([
            self.z_copy(0, 0, d, part(lax.rem(self.z + d, self.nz)), self.a1.at[self.z]) for d in far_first(self.nz)
        ])
        self.a1[self.z] = part(self.z)[...]
        return copies

    def a_mid(self, arriving):
        for copy in arriving:
            copy.wait_recv()
        height = self.rows // self.nz // NY

        def part(q):
            return self.a1.at[:, pl.ds(pl.multiple_of(q * height, 8), height)]

        copies = self.begin([
            self.y_copy(0, 0, d, part(lax.rem(self.y + d, NY)), self.a2.at[self.y]) for d in (2, 1, 3)
        ])
        self.a2[self.y] = part(self.y)[...]
        return copies

    def a_back(self, arriving):
        for copy in arriving:
            copy.wait_recv()
        order = [(j, i) for j in range(self.nz) for i in range(NY)]
        total = jnp.zeros(self.a2.shape[2:], F32)
        for j, i in reversed(order) if self.reverse else order:
            self.a3[i, j] = total
            total = total + self.a2[i, j]
        copies = self.begin([
            self.y_copy(1, 0, d, self.a3.at[lax.rem(self.y + d, NY)], self.a4.at[self.y]) for d in (2, 1, 3)
        ])
        self.a4[self.y] = self.a3[self.y]
        return copies

    def a_end(self, arriving):
        for copy in arriving:
            copy.wait_recv()
        copies = self.begin([
            self.z_copy(1, 0, d, self.a4.at[:, lax.rem(self.z + d, self.nz)], self.a5.at[self.z])
            for d in far_first(self.nz)
        ])
        self.a5[self.z] = self.a4[:, self.z]
        return copies

    def first(self, c):
        return self.a_out() if c == 0 else self.y_out(c)

    def second(self, moving):
        for c in (1, 2, 0, 3):
            moving[c] = self.a_mid(moving[c]) if c == 0 else self.z_out(c, moving[c])

    def third(self, moving):
        for c in (1, 0, 2, 3):
            moving[c] = self.a_back(moving[c]) if c == 0 else self.z_back(c, moving[c])

    def fourth(self, moving):
        for c in (0, 1, 2, 3):
            moving[c] = self.a_end(moving[c]) if c == 0 else self.y_back(c, moving[c])

    def result(self, c, arriving):
        for copy in arriving:
            copy.wait_recv()
        return (self.a5[...] if c == 0 else self.b4[c]).reshape(self.rows, HD).astype(BF16)

    def finish(self):
        for copy in self.sends:
            copy.wait_send()


def lanes(h):
    return pl.ds(pl.multiple_of(h * HD, HD), HD)


def sub(h):
    return pl.ds(pl.multiple_of(h * HD, HD), HD)


def each(first, count, body):
    def step(h, _):
        body(h)
        return 0

    lax.fori_loop(first, first + count, step, 0)


def kernel(nz, nh, heads, q_hbm, k_hbm, v_hbm, gain_hbm, g_hbm, normed, qgrad, kgrad, vgrad, kpart_end, vpart_end,
           later_end, k_end, v_end, q, k, v, gain, g, grad_norm, scores, att, dout, kpart, vpart, state_bf, squares,
           products, inv_b, coef_b, head_src, head_dst, *rest):
    fwd_refs, bwd_refs = rest[0:13], rest[13:26]
    fwd_sems, bwd_sems = rest[26:30], rest[30:34]
    in_sem, head_send, head_recv = rest[34:37]
    scale = HD ** (-0.5)
    per = heads // CHUNKS
    rows = per * HD
    width = heads * HD
    seq, head = lax.axis_index("seq"), lax.axis_index("head")
    z, y = lax.div(seq, NY), lax.rem(seq, NY)

    loads = []

    def load(c):
        cols = pl.ds(c * rows, rows)
        pair = []
        for i, (src, dst) in enumerate(((k_hbm, k), (v_hbm, v))):
            copy = pltpu.make_async_copy(src.at[:, cols], dst.at[:, cols], in_sem.at[2 * c + i])
            copy.start()
            pair.append(copy)
        loads.append(pair)

    load(0)
    barrier = pltpu.get_barrier_semaphore()
    for d in far_first(nz):
        to = lax.rem(z + d, nz) * NY + y
        pl.semaphore_signal(barrier, inc=1, device_id=(to, head), device_id_type=MESH)
    for d in range(1, nh):
        pl.semaphore_signal(barrier, inc=1, device_id=(seq, lax.rem(head + d, nh)), device_id_type=MESH)
    for d in far_first(NY):
        to = z * NY + lax.rem(y + d, NY)
        pl.semaphore_signal(barrier, inc=1, device_id=(to, head), device_id_type=MESH)

    for c in range(1, CHUNKS):
        load(c)
    late = []
    for i, (src, dst) in enumerate(((q_hbm, q), (g_hbm, g), (gain_hbm, gain))):
        copy = pltpu.make_async_copy(src, dst, in_sem.at[2 * CHUNKS + i])
        copy.start()
        late.append(copy)

    fwd = Scan(nz, rows, False, fwd_refs, fwd_sems)
    bwd = Scan(nz, rows, True, bwd_refs, bwd_sems)

    def kv(h):
        fwd.block[sub(h), :] = dot_tn(k[:, lanes(h)], v[:, lanes(h)])

    moving = []
    for c in range(CHUNKS):
        for copy in loads[c]:
            copy.wait()
        for h in range(c * per, (c + 1) * per):
            kv(h)
        if c == 0:
            pl.semaphore_wait(barrier, (NY - 1) + (nz - 1) + (nh - 1))
        moving.append(fwd.first(c))
    for copy in late:
        copy.wait()

    causal = lax.broadcasted_iota(jnp.int32, (HALF, HALF), 0) >= lax.broadcasted_iota(jnp.int32, (HALF, HALF), 1)

    def tiles(a, b, factor):
        top = jnp.where(causal, dot_nt(a[:HALF], b[:HALF]) * factor, 0.0).astype(BF16)
        low = (dot_nt(a[HALF:], b[:HALF]) * factor).astype(BF16)
        end = jnp.where(causal, dot_nt(a[HALF:], b[HALF:]) * factor, 0.0).astype(BF16)
        return top, low, end

    def intra(h):
        vh = v[:, lanes(h)]
        top, low, end = tiles(q[:, lanes(h)], k[:, lanes(h)], scale)
        scores[h, 0], scores[h, 1], scores[h, 2] = top, low, end
        att[:HALF, lanes(h)] = dot_nn(top, vh[:HALF])
        att[HALF:, lanes(h)] = dot_nn(low, vh[:HALF]) + dot_nn(end, vh[HALF:])
        grad_norm[:, lanes(h)] = g[:, lanes(h)].astype(F32) * gain[:, lanes(h)]

    each(0, AHEAD[0], intra)
    fwd.second(moving)
    each(AHEAD[0], AHEAD[1], intra)
    fwd.third(moving)
    each(AHEAD[0] + AHEAD[1], heads - AHEAD[0] - AHEAD[1], intra)
    fwd.fourth(moving)
    for c in ARRIVAL:
        here = fwd.result(c, moving[c])
        state_bf[pl.ds(c * rows, rows), :] = here
        sq, pr = (0.0, 0.0) if c == ARRIVAL[0] else (squares[...], products[...])
        for i in range(per):
            h = c * per + i
            a = att[:, lanes(h)] + scale * dot_nn(q[:, lanes(h)], here[i * HD : (i + 1) * HD])
            att[:, lanes(h)] = a
            sq = sq + a * a
            pr = pr + a * grad_norm[:, lanes(h)]
        squares[...], products[...] = sq, pr

    row = lax.broadcasted_iota(jnp.int32, (8, HD), 0)
    groups = BLK // HD
    packed = jnp.zeros((8, HD), F32)
    for t in range(groups):
        part = pl.ds(t * HD, HD)
        for first, totals in ((0, squares), (groups, products)):
            pick = (row == first + t).astype(BF16)
            packed = packed + dot_nt(
                jnp.concatenate([pick, pick], axis=1), jnp.concatenate(split(totals[part, :], 2), axis=1)
            )
    head_src[...] = packed
    head_copies = []
    for d in range(1, nh):
        copy = pltpu.make_async_remote_copy(
            src_ref=head_src, dst_ref=head_dst.at[head], send_sem=head_send.at[d - 1], recv_sem=head_recv.at[d - 1],
            device_id=(seq, lax.rem(head + d, nh)), device_id_type=MESH,
        )
        copy.start()
        head_copies.append(copy)
    head_dst[head] = packed
    for copy in head_copies:
        copy.wait_recv()
    sums = head_dst[0]
    for j in range(1, nh):
        sums = sums + head_dst[j]
    full = nh * width
    inv = 1.0 / jnp.sqrt(sums[:groups] / full + 1e-06)
    proj = (sums[groups:] * inv) / full
    both = jnp.concatenate(split(jnp.concatenate([inv, (inv * proj) * inv], axis=0), 3), axis=0)
    for t in range(groups):
        part = pl.ds(t * HD, HD)
        for first, spread in ((0, inv_b), (groups, coef_b)):
            pick = (row == first + t).astype(BF16)
            spread[part, :] = dot_tn(both, jnp.concatenate([pick, pick, pick], axis=0))

    def grad(h):
        d = (grad_norm[:, lanes(h)] * inv_b[...] - att[:, lanes(h)] * coef_b[...]).astype(BF16)
        dout[:, lanes(h)] = d
        bwd.block[sub(h), :] = dot_tn(q[:, lanes(h)], d)

    for c in range(CHUNKS):
        for h in range(c * per, (c + 1) * per):
            grad(h)
        moving[c] = bwd.first(c)

    def back(h):
        qh, kh, vh, d = q[:, lanes(h)], k[:, lanes(h)], v[:, lanes(h)], dout[:, lanes(h)]
        normed[:, lanes(h)] = (att[:, lanes(h)] * inv_b[...] * gain[:, lanes(h)]).astype(BF16)
        top, low, end = tiles(d, vh, 1.0)
        carried = dot_nt(d, state_bf[sub(h), :])
        qgrad[:HALF, lanes(h)] = (scale * (dot_nn(top, kh[:HALF]) + carried[:HALF])).astype(BF16)
        qgrad[HALF:, lanes(h)] = (
            scale * (dot_nn(low, kh[:HALF]) + dot_nn(end, kh[HALF:]) + carried[HALF:])
        ).astype(BF16)
        kpart[:HALF, lanes(h)] = dot_tn(top, qh[:HALF]) + dot_tn(low, qh[HALF:])
        kpart[HALF:, lanes(h)] = dot_tn(end, qh[HALF:])
        vpart[:HALF, lanes(h)] = dot_tn(scores[h, 0], d[:HALF]) + dot_tn(scores[h, 1], d[HALF:])
        vpart[HALF:, lanes(h)] = dot_tn(scores[h, 2], d[HALF:])

    done = 0
    each(done, BEHIND[0], back)
    done += BEHIND[0]
    bwd.second(moving)
    each(done, BEHIND[1], back)
    done += BEHIND[1]
    bwd.third(moving)
    each(done, BEHIND[2], back)
    done += BEHIND[2]
    early, bwd.sends = bwd.sends, []
    bwd.fourth(moving)
    each(done, heads - done, back)
    fwd.finish()
    for copy in head_copies + early:
        copy.wait_send()
    end = pl.ds((CHUNKS - 1) * rows, rows)
    k_end[...], v_end[...] = k[:, end], v[:, end]
    kpart_end[...], vpart_end[...] = kpart[:, end], vpart[:, end]
    for c in ARRIVAL:
        here = bwd.result(c, moving[c])
        if c == CHUNKS - 1:
            later_end[...] = here
            break
        for i in range(per):
            h = c * per + i
            one = here[i * HD : (i + 1) * HD]
            kgrad[:, lanes(h)] = (scale * (kpart[:, lanes(h)] + dot_nt(v[:, lanes(h)], one))).astype(BF16)
            vgrad[:, lanes(h)] = (vpart[:, lanes(h)] + scale * dot_nn(k[:, lanes(h)], one)).astype(BF16)

    bwd.finish()


def finish_kernel(per, normed, qgrad, kgrad, vgrad, kpart, vpart, later, k, v, normed_hbm, qgrad_hbm, kgrad_hbm,
                  vgrad_hbm, kgrad_end, vgrad_end, out_sem):
    scale = HD ** (-0.5)
    outs = []

    def put(src, dst):
        copy = pltpu.make_async_copy(src, dst, out_sem.at[len(outs)])
        copy.start()
        outs.append(copy)

    begun = kgrad.shape[1] - per * HD
    for src, dst in ((kgrad, kgrad_hbm), (vgrad, vgrad_hbm)):
        put(src.at[:, pl.ds(0, begun)], dst.at[:, pl.ds(0, begun)])
    put(normed, normed_hbm)
    put(qgrad, qgrad_hbm)
    for h in range(per):
        kgrad_end[:, lanes(h)] = (scale * (kpart[:, lanes(h)] + dot_nt(v[:, lanes(h)], later[sub(h), :]))).astype(BF16)
        vgrad_end[:, lanes(h)] = (vpart[:, lanes(h)] + scale * dot_nn(k[:, lanes(h)], later[sub(h), :])).astype(BF16)
    for src, dst in ((kgrad_end, kgrad_hbm), (vgrad_end, vgrad_hbm)):
        put(src, dst.at[:, pl.ds(begun, per * HD)])
    for copy in outs:
        copy.wait()


def local(queries, keys, values, norm_gain, out_grad):
    blk, width = queries.shape
    heads = width // HD
    nz = lax.axis_size("seq") // NY
    nh = lax.axis_size("head")
    rows = heads // CHUNKS * HD
    quarter = rows // NY
    piece = quarter // nz
    vmem = pltpu.VMEM

    def scan_refs():
        return [
            vmem((heads * HD, HD), F32),
            vmem((CHUNKS, NY, quarter, HD), F32),
            vmem((CHUNKS, quarter, HD), F32),
            vmem((CHUNKS, nz, piece, HD), F32),
            vmem((CHUNKS, nz, piece, HD), F32),
            vmem((CHUNKS, nz, piece, HD), F32),
            vmem((CHUNKS, NY, quarter, HD), F32),
            vmem((CHUNKS, NY, quarter, HD), F32),
            vmem((nz, rows // nz, HD), F32),
            vmem((NY, nz, rows // nz // NY, HD), F32),
            vmem((NY, nz, rows // nz // NY, HD), F32),
            vmem((NY, nz, rows // nz // NY, HD), F32),
            vmem((nz, NY, rows // nz // NY, HD), F32),
        ]

    def scan_sems():
        y, zz = 2 * CHUNKS * (NY - 1), 2 * CHUNKS * (nz - 1)
        dma = pltpu.SemaphoreType.DMA
        return [dma((y,)), dma((y,)), dma((zz,)), dma((zz,))]

    big_f32, big_bf16 = vmem((blk, width), F32), vmem((blk, width), BF16)
    end_f32, end_bf16 = vmem((blk, rows), F32), vmem((blk, rows), BF16)
    scratch = [
        big_bf16, big_bf16, big_bf16, vmem((1, width), F32), big_bf16, big_f32,
        vmem((heads, 3, HALF, HALF), BF16),
        big_f32, big_bf16, big_f32, big_f32,
        vmem((heads * HD, HD), BF16),
        vmem((blk, HD), F32), vmem((blk, HD), F32), vmem((blk, HD), F32), vmem((blk, HD), F32),
        vmem((8, HD), F32), vmem((nh, 8, HD), F32),
        *scan_refs(), *scan_refs(), *scan_sems(), *scan_sems(),
        pltpu.SemaphoreType.DMA((2 * CHUNKS + 3,)),
        pltpu.SemaphoreType.DMA((nh - 1,)),
        pltpu.SemaphoreType.DMA((nh - 1,)),
    ]
    out = jax.ShapeDtypeStruct((blk, width), BF16)
    anywhere, in_vmem = pl.BlockSpec(memory_space=pl.ANY), pl.BlockSpec(memory_space=pltpu.VMEM)
    parts = pl.pallas_call(
        functools.partial(kernel, nz, nh, heads),
        out_shape=(
            big_bf16, big_bf16, big_bf16, big_bf16, end_f32, end_f32, vmem((rows, HD), BF16), end_bf16, end_bf16,
        ),
        in_specs=[anywhere] * 5,
        out_specs=(in_vmem,) * 9,
        scratch_shapes=scratch,
        compiler_params=pltpu.CompilerParams(
            collective_id=0, has_side_effects=True, vmem_limit_bytes=40 * 1024 * 1024
        ),
        name="linear_attention",
    )(*[
        pltpu.with_memory_space_constraint(a, pltpu.HBM)
        for a in (queries, keys, values, norm_gain.reshape(1, width), out_grad)
    ])
    return pl.pallas_call(
        functools.partial(finish_kernel, heads // CHUNKS),
        out_shape=(out,) * 4,
        in_specs=[in_vmem] * 9,
        out_specs=(anywhere,) * 4,
        scratch_shapes=[end_bf16, end_bf16, pltpu.SemaphoreType.DMA((6,))],
        compiler_params=pltpu.CompilerParams(vmem_limit_bytes=28 * 1024 * 1024),
        name="key_value_grads",
    )(*parts)


def solution(mesh):
    placed = (P("seq", "head"), P("seq", "head"), P("seq", "head"), P("head"), P("seq", "head"))
    return jax.shard_map(
        local,
        mesh=mesh,
        in_specs=placed,
        out_specs=(P("seq", "head"), P("seq", "head"), P("seq", "head"), P("seq", "head")),
        check_vma=False,
    )
```

```python
import functools

import jax
import jax.numpy as jnp
from jax import lax
from jax.experimental import pallas as pl
from jax.experimental.pallas import tpu as pltpu
from jax.sharding import PartitionSpec as P

HD = 128
BLK = 512
NY = 4
CHUNKS = 4
ORDER = (1, 2, 0, 3)
ARRIVAL = (1, 2, 0, 3)
AHEAD = (3, 3)
BEHIND = (2, 2, 2)
HALF = BLK // 2
F32 = jnp.float32
BF16 = jnp.bfloat16
MESH = pl.DeviceIdType.MESH


def dot_nn(a, b):
    return lax.dot_general(a, b, (((1,), (0,)), ((), ())), preferred_element_type=F32)


def dot_nt(a, b):
    return lax.dot_general(a, b, (((1,), (1,)), ((), ())), preferred_element_type=F32)


def dot_tn(a, b):
    return lax.dot_general(a, b, (((0,), (0,)), ((), ())), preferred_element_type=F32)


def split(a, count):
    parts = []
    for _ in range(count):
        parts.append(a.astype(BF16))
        a = a - parts[-1].astype(F32)
    return parts


def far_first(count):
    return sorted(range(1, count), key=lambda d: -min(d, count - d))


class Scan:
    def __init__(self, nz, rows, reverse, refs, sems):
        self.nz, self.rows, self.reverse = nz, rows, reverse
        self.block, self.b1, self.tot, self.b2, self.pre, self.b3, self.ret, self.b4 = refs[:8]
        self.a1, self.a2, self.a3, self.a4, self.a5 = refs[8:]
        self.ysend, self.yrecv, self.zsend, self.zrecv = sems
        seq = lax.axis_index("seq")
        self.head = lax.axis_index("head")
        self.z, self.y = lax.div(seq, NY), lax.rem(seq, NY)
        self.quarter = rows // NY
        self.piece = self.quarter // nz
        self.sends = []

    def y_copy(self, phase, c, d, src, dst):
        k = (phase * CHUNKS + c) * (NY - 1) + d - 1
        to = self.z * NY + lax.rem(self.y + d, NY)
        return pltpu.make_async_remote_copy(
            src_ref=src, dst_ref=dst, send_sem=self.ysend.at[k], recv_sem=self.yrecv.at[k],
            device_id=(to, self.head), device_id_type=MESH,
        )

    def z_copy(self, phase, c, d, src, dst):
        k = (phase * CHUNKS + c) * (self.nz - 1) + d - 1
        to = lax.rem(self.z + d, self.nz) * NY + self.y
        return pltpu.make_async_remote_copy(
            src_ref=src, dst_ref=dst, send_sem=self.zsend.at[k], recv_sem=self.zrecv.at[k],
            device_id=(to, self.head), device_id_type=MESH,
        )

    def begin(self, copies):
        for copy in copies:
            copy.start()
        self.sends += copies
        return copies

    def y_out(self, c):
        base = c * self.rows

        def part(q):
            return self.block.at[pl.ds(pl.multiple_of(base + q * self.quarter, 8), self.quarter)]

        copies = self.begin([
            self.y_copy(0, c, d, part(lax.rem(self.y + d, NY)), self.b1.at[c, self.y]) for d in (2, 1, 3)
        ])
        self.b1[c, self.y] = part(self.y)[...]
        return copies

    def z_out(self, c, arriving):
        for copy in arriving:
            copy.wait_recv()
        self.tot[c] = (self.b1[c, 0] + self.b1[c, 1]) + (self.b1[c, 2] + self.b1[c, 3])

        def part(j):
            return self.tot.at[c, pl.ds(pl.multiple_of(j * self.piece, 8), self.piece)]

        copies = self.begin([
            self.z_copy(0, c, d, part(lax.rem(self.z + d, self.nz)), self.b2.at[c, self.z]) for d in far_first(self.nz)
        ])
        self.b2[c, self.z] = part(self.z)[...]
        return copies

    def z_back(self, c, arriving):
        for copy in arriving:
            copy.wait_recv()
        order = range(self.nz)
        total = jnp.zeros((self.piece, HD), F32)
        for j in reversed(order) if self.reverse else order:
            self.pre[c, j] = total
            total = total + self.b2[c, j]
        copies = self.begin([
            self.z_copy(1, c, d, self.pre.at[c, lax.rem(self.z + d, self.nz)], self.b3.at[c, self.z]) for d in far_first(self.nz)
        ])
        self.b3[c, self.z] = self.pre[c, self.z]
        return copies

    def y_back(self, c, arriving):
        for copy in arriving:
            copy.wait_recv()
        total = self.b3[c].reshape(self.quarter, HD)
        order = range(NY)
        for j in reversed(order) if self.reverse else order:
            self.ret[c, j] = total
            total = total + self.b1[c, j]
        copies = self.begin([
            self.y_copy(1, c, d, self.ret.at[c, lax.rem(self.y + d, NY)], self.b4.at[c, self.y]) for d in (2, 1, 3)
        ])
        self.b4[c, self.y] = self.ret[c, self.y]
        return copies

    def a_out(self):
        height = self.rows // self.nz

        def part(j):
            return self.block.at[pl.ds(pl.multiple_of(j * height, 8), height)]

        copies = self.begin([
            self.z_copy(0, 0, d, part(lax.rem(self.z + d, self.nz)), self.a1.at[self.z]) for d in far_first(self.nz)
        ])
        self.a1[self.z] = part(self.z)[...]
        return copies

    def a_mid(self, arriving):
        for copy in arriving:
            copy.wait_recv()
        height = self.rows // self.nz // NY

        def part(q):
            return self.a1.at[:, pl.ds(pl.multiple_of(q * height, 8), height)]

        copies = self.begin([
            self.y_copy(0, 0, d, part(lax.rem(self.y + d, NY)), self.a2.at[self.y]) for d in (2, 1, 3)
        ])
        self.a2[self.y] = part(self.y)[...]
        return copies

    def a_back(self, arriving):
        for copy in arriving:
            copy.wait_recv()
        order = [(j, i) for j in range(self.nz) for i in range(NY)]
        total = jnp.zeros(self.a2.shape[2:], F32)
        for j, i in reversed(order) if self.reverse else order:
            self.a3[i, j] = total
            total = total + self.a2[i, j]
        copies = self.begin([
            self.y_copy(1, 0, d, self.a3.at[lax.rem(self.y + d, NY)], self.a4.at[self.y]) for d in (2, 1, 3)
        ])
        self.a4[self.y] = self.a3[self.y]
        return copies

    def a_end(self, arriving):
        for copy in arriving:
            copy.wait_recv()
        copies = self.begin([
            self.z_copy(1, 0, d, self.a4.at[:, lax.rem(self.z + d, self.nz)], self.a5.at[self.z])
            for d in far_first(self.nz)
        ])
        self.a5[self.z] = self.a4[:, self.z]
        return copies

    def first(self, c):
        return self.a_out() if c == 0 else self.y_out(c)

    def second(self, moving):
        for c in (1, 2, 0, 3):
            moving[c] = self.a_mid(moving[c]) if c == 0 else self.z_out(c, moving[c])

    def third(self, moving):
        for c in (0, 1, 2, 3):
            moving[c] = self.a_back(moving[c]) if c == 0 else self.z_back(c, moving[c])

    def fourth(self, moving):
        for c in (0, 1, 2, 3):
            moving[c] = self.a_end(moving[c]) if c == 0 else self.y_back(c, moving[c])

    def result(self, c, arriving):
        for copy in arriving:
            copy.wait_recv()
        return (self.a5[...] if c == 0 else self.b4[c]).reshape(self.rows, HD).astype(BF16)

    def finish(self):
        for copy in self.sends:
            copy.wait_send()


def lanes(h):
    return pl.ds(pl.multiple_of(h * HD, HD), HD)


def sub(h):
    return pl.ds(pl.multiple_of(h * HD, HD), HD)


def each(first, count, body):
    def step(h, _):
        body(h)
        return 0

    lax.fori_loop(first, first + count, step, 0)


def kernel(nz, nh, heads, q_hbm, k_hbm, v_hbm, gain_hbm, g_hbm, normed, qgrad, kgrad, vgrad, kpart_end, vpart_end,
           later_end, k_end, v_end, q, k, v, gain, g, grad_norm, scores, att, dout, kpart, vpart, state_bf, squares,
           products, inv_b, coef_b, head_src, head_dst, *rest):
    fwd_refs, bwd_refs = rest[0:13], rest[13:26]
    fwd_sems, bwd_sems = rest[26:30], rest[30:34]
    in_sem, head_send, head_recv = rest[34:37]
    scale = HD ** (-0.5)
    per = heads // CHUNKS
    rows = per * HD
    width = heads * HD
    seq, head = lax.axis_index("seq"), lax.axis_index("head")
    z, y = lax.div(seq, NY), lax.rem(seq, NY)

    loads = []

    def load(c):
        cols = pl.ds(c * rows, rows)
        pair = []
        for i, (src, dst) in enumerate(((k_hbm, k), (v_hbm, v))):
            copy = pltpu.make_async_copy(src.at[:, cols], dst.at[:, cols], in_sem.at[2 * c + i])
            copy.start()
            pair.append(copy)
        loads.append(pair)

    load(0)
    barrier = pltpu.get_barrier_semaphore()
    for d in far_first(nz):
        to = lax.rem(z + d, nz) * NY + y
        pl.semaphore_signal(barrier, inc=1, device_id=(to, head), device_id_type=MESH)
    for d in range(1, nh):
        pl.semaphore_signal(barrier, inc=1, device_id=(seq, lax.rem(head + d, nh)), device_id_type=MESH)
    for d in far_first(NY):
        to = z * NY + lax.rem(y + d, NY)
        pl.semaphore_signal(barrier, inc=1, device_id=(to, head), device_id_type=MESH)

    for c in range(1, CHUNKS):
        load(c)
    late = []
    for i, (src, dst) in enumerate(((q_hbm, q), (g_hbm, g), (gain_hbm, gain))):
        copy = pltpu.make_async_copy(src, dst, in_sem.at[2 * CHUNKS + i])
        copy.start()
        late.append(copy)

    fwd = Scan(nz, rows, False, fwd_refs, fwd_sems)
    bwd = Scan(nz, rows, True, bwd_refs, bwd_sems)

    def kv(h):
        fwd.block[sub(h), :] = dot_tn(k[:, lanes(h)], v[:, lanes(h)])

    moving = []
    for c in range(CHUNKS):
        for copy in loads[c]:
            copy.wait()
        for h in range(c * per, (c + 1) * per):
            kv(h)
        if c == 0:
            pl.semaphore_wait(barrier, (NY - 1) + (nz - 1) + (nh - 1))
        moving.append(fwd.first(c))
    for copy in late:
        copy.wait()

    causal = lax.broadcasted_iota(jnp.int32, (HALF, HALF), 0) >= lax.broadcasted_iota(jnp.int32, (HALF, HALF), 1)

    def tiles(a, b, factor):
        top = jnp.where(causal, dot_nt(a[:HALF], b[:HALF]) * factor, 0.0).astype(BF16)
        low = (dot_nt(a[HALF:], b[:HALF]) * factor).astype(BF16)
        end = jnp.where(causal, dot_nt(a[HALF:], b[HALF:]) * factor, 0.0).astype(BF16)
        return top, low, end

    def intra(h):
        vh = v[:, lanes(h)]
        top, low, end = tiles(q[:, lanes(h)], k[:, lanes(h)], scale)
        scores[h, 0], scores[h, 1], scores[h, 2] = top, low, end
        att[:HALF, lanes(h)] = dot_nn(top, vh[:HALF])
        att[HALF:, lanes(h)] = dot_nn(low, vh[:HALF]) + dot_nn(end, vh[HALF:])
        grad_norm[:, lanes(h)] = g[:, lanes(h)].astype(F32) * gain[:, lanes(h)]

    each(0, AHEAD[0], intra)
    fwd.second(moving)
    each(AHEAD[0], AHEAD[1], intra)
    fwd.third(moving)
    each(AHEAD[0] + AHEAD[1], heads - AHEAD[0] - AHEAD[1], intra)
    fwd.fourth(moving)
    for c in ARRIVAL:
        here = fwd.result(c, moving[c])
        state_bf[pl.ds(c * rows, rows), :] = here
        sq, pr = (0.0, 0.0) if c == ARRIVAL[0] else (squares[...], products[...])
        for i in range(per):
            h = c * per + i
            a = att[:, lanes(h)] + scale * dot_nn(q[:, lanes(h)], here[i * HD : (i + 1) * HD])
            att[:, lanes(h)] = a
            sq = sq + a * a
            pr = pr + a * grad_norm[:, lanes(h)]
        squares[...], products[...] = sq, pr

    row = lax.broadcasted_iota(jnp.int32, (8, HD), 0)
    groups = BLK // HD
    packed = jnp.zeros((8, HD), F32)
    for t in range(groups):
        part = pl.ds(t * HD, HD)
        for first, totals in ((0, squares), (groups, products)):
            pick = (row == first + t).astype(BF16)
            packed = packed + dot_nt(
                jnp.concatenate([pick, pick], axis=1), jnp.concatenate(split(totals[part, :], 2), axis=1)
            )
    head_src[...] = packed
    head_copies = []
    for d in far_first(nh):
        copy = pltpu.make_async_remote_copy(
            src_ref=head_src, dst_ref=head_dst.at[head], send_sem=head_send.at[d - 1], recv_sem=head_recv.at[d - 1],
            device_id=(seq, lax.rem(head + d, nh)), device_id_type=MESH,
        )
        copy.start()
        head_copies.append(copy)
    head_dst[head] = packed
    for copy in head_copies:
        copy.wait_recv()
    sums = head_dst[0]
    for j in range(1, nh):
        sums = sums + head_dst[j]
    full = nh * width
    inv = 1.0 / jnp.sqrt(sums[:groups] / full + 1e-06)
    proj = (sums[groups:] * inv) / full
    both = jnp.concatenate(split(jnp.concatenate([inv, (inv * proj) * inv], axis=0), 3), axis=0)
    for t in range(groups):
        part = pl.ds(t * HD, HD)
        for first, spread in ((0, inv_b), (groups, coef_b)):
            pick = (row == first + t).astype(BF16)
            spread[part, :] = dot_tn(both, jnp.concatenate([pick, pick, pick], axis=0))

    def grad(h):
        d = (grad_norm[:, lanes(h)] * inv_b[...] - att[:, lanes(h)] * coef_b[...]).astype(BF16)
        dout[:, lanes(h)] = d
        bwd.block[sub(h), :] = dot_tn(q[:, lanes(h)], d)

    for c in range(CHUNKS):
        for h in range(c * per, (c + 1) * per):
            grad(h)
        moving[c] = bwd.first(c)

    def back(h):
        qh, kh, vh, d = q[:, lanes(h)], k[:, lanes(h)], v[:, lanes(h)], dout[:, lanes(h)]
        normed[:, lanes(h)] = (att[:, lanes(h)] * inv_b[...] * gain[:, lanes(h)]).astype(BF16)
        top, low, end = tiles(d, vh, 1.0)
        carried = dot_nt(d, state_bf[sub(h), :])
        qgrad[:HALF, lanes(h)] = (scale * (dot_nn(top, kh[:HALF]) + carried[:HALF])).astype(BF16)
        qgrad[HALF:, lanes(h)] = (
            scale * (dot_nn(low, kh[:HALF]) + dot_nn(end, kh[HALF:]) + carried[HALF:])
        ).astype(BF16)
        kpart[:HALF, lanes(h)] = dot_tn(top, qh[:HALF]) + dot_tn(low, qh[HALF:])
        kpart[HALF:, lanes(h)] = dot_tn(end, qh[HALF:])
        vpart[:HALF, lanes(h)] = dot_tn(scores[h, 0], d[:HALF]) + dot_tn(scores[h, 1], d[HALF:])
        vpart[HALF:, lanes(h)] = dot_tn(scores[h, 2], d[HALF:])

    done = 0
    each(done, BEHIND[0], back)
    done += BEHIND[0]
    bwd.second(moving)
    each(done, BEHIND[1], back)
    done += BEHIND[1]
    bwd.third(moving)
    each(done, BEHIND[2], back)
    done += BEHIND[2]
    early, bwd.sends = bwd.sends, []
    bwd.fourth(moving)
    each(done, heads - done, back)
    fwd.finish()
    for copy in head_copies + early:
        copy.wait_send()
    end = pl.ds((CHUNKS - 1) * rows, rows)
    k_end[...], v_end[...] = k[:, end], v[:, end]
    kpart_end[...], vpart_end[...] = kpart[:, end], vpart[:, end]
    for c in ARRIVAL:
        here = bwd.result(c, moving[c])
        if c == CHUNKS - 1:
            later_end[...] = here
            break
        for i in range(per):
            h = c * per + i
            one = here[i * HD : (i + 1) * HD]
            kgrad[:, lanes(h)] = (scale * (kpart[:, lanes(h)] + dot_nt(v[:, lanes(h)], one))).astype(BF16)
            vgrad[:, lanes(h)] = (vpart[:, lanes(h)] + scale * dot_nn(k[:, lanes(h)], one)).astype(BF16)

    bwd.finish()


def finish_kernel(per, normed, qgrad, kgrad, vgrad, kpart, vpart, later, k, v, normed_hbm, qgrad_hbm, kgrad_hbm,
                  vgrad_hbm, kgrad_end, vgrad_end, out_sem):
    scale = HD ** (-0.5)
    outs = []

    def put(src, dst):
        copy = pltpu.make_async_copy(src, dst, out_sem.at[len(outs)])
        copy.start()
        outs.append(copy)

    begun = kgrad.shape[1] - per * HD
    for src, dst in ((kgrad, kgrad_hbm), (vgrad, vgrad_hbm)):
        put(src.at[:, pl.ds(0, begun)], dst.at[:, pl.ds(0, begun)])
    put(normed, normed_hbm)
    put(qgrad, qgrad_hbm)
    for h in range(per):
        kgrad_end[:, lanes(h)] = (scale * (kpart[:, lanes(h)] + dot_nt(v[:, lanes(h)], later[sub(h), :]))).astype(BF16)
        vgrad_end[:, lanes(h)] = (vpart[:, lanes(h)] + scale * dot_nn(k[:, lanes(h)], later[sub(h), :])).astype(BF16)
    for src, dst in ((kgrad_end, kgrad_hbm), (vgrad_end, vgrad_hbm)):
        put(src, dst.at[:, pl.ds(begun, per * HD)])
    for copy in outs:
        copy.wait()


def local(queries, keys, values, norm_gain, out_grad):
    blk, width = queries.shape
    heads = width // HD
    nz = lax.axis_size("seq") // NY
    nh = lax.axis_size("head")
    rows = heads // CHUNKS * HD
    quarter = rows // NY
    piece = quarter // nz
    vmem = pltpu.VMEM

    def scan_refs():
        return [
            vmem((heads * HD, HD), F32),
            vmem((CHUNKS, NY, quarter, HD), F32),
            vmem((CHUNKS, quarter, HD), F32),
            vmem((CHUNKS, nz, piece, HD), F32),
            vmem((CHUNKS, nz, piece, HD), F32),
            vmem((CHUNKS, nz, piece, HD), F32),
            vmem((CHUNKS, NY, quarter, HD), F32),
            vmem((CHUNKS, NY, quarter, HD), F32),
            vmem((nz, rows // nz, HD), F32),
            vmem((NY, nz, rows // nz // NY, HD), F32),
            vmem((NY, nz, rows // nz // NY, HD), F32),
            vmem((NY, nz, rows // nz // NY, HD), F32),
            vmem((nz, NY, rows // nz // NY, HD), F32),
        ]

    def scan_sems():
        y, zz = 2 * CHUNKS * (NY - 1), 2 * CHUNKS * (nz - 1)
        dma = pltpu.SemaphoreType.DMA
        return [dma((y,)), dma((y,)), dma((zz,)), dma((zz,))]

    big_f32, big_bf16 = vmem((blk, width), F32), vmem((blk, width), BF16)
    end_f32, end_bf16 = vmem((blk, rows), F32), vmem((blk, rows), BF16)
    scratch = [
        big_bf16, big_bf16, big_bf16, vmem((1, width), F32), big_bf16, big_f32,
        vmem((heads, 3, HALF, HALF), BF16),
        big_f32, big_bf16, big_f32, big_f32,
        vmem((heads * HD, HD), BF16),
        vmem((blk, HD), F32), vmem((blk, HD), F32), vmem((blk, HD), F32), vmem((blk, HD), F32),
        vmem((8, HD), F32), vmem((nh, 8, HD), F32),
        *scan_refs(), *scan_refs(), *scan_sems(), *scan_sems(),
        pltpu.SemaphoreType.DMA((2 * CHUNKS + 3,)),
        pltpu.SemaphoreType.DMA((nh - 1,)),
        pltpu.SemaphoreType.DMA((nh - 1,)),
    ]
    out = jax.ShapeDtypeStruct((blk, width), BF16)
    anywhere, in_vmem = pl.BlockSpec(memory_space=pl.ANY), pl.BlockSpec(memory_space=pltpu.VMEM)
    parts = pl.pallas_call(
        functools.partial(kernel, nz, nh, heads),
        out_shape=(
            big_bf16, big_bf16, big_bf16, big_bf16, end_f32, end_f32, vmem((rows, HD), BF16), end_bf16, end_bf16,
        ),
        in_specs=[anywhere] * 5,
        out_specs=(in_vmem,) * 9,
        scratch_shapes=scratch,
        compiler_params=pltpu.CompilerParams(
            collective_id=0, has_side_effects=True, vmem_limit_bytes=40 * 1024 * 1024
        ),
        name="linear_attention",
    )(*[
        pltpu.with_memory_space_constraint(a, pltpu.HBM)
        for a in (queries, keys, values, norm_gain.reshape(1, width), out_grad)
    ])
    return pl.pallas_call(
        functools.partial(finish_kernel, heads // CHUNKS),
        out_shape=(out,) * 4,
        in_specs=[in_vmem] * 9,
        out_specs=(anywhere,) * 4,
        scratch_shapes=[end_bf16, end_bf16, pltpu.SemaphoreType.DMA((6,))],
        compiler_params=pltpu.CompilerParams(vmem_limit_bytes=28 * 1024 * 1024),
        name="key_value_grads",
    )(*parts)


def solution(mesh):
    placed = (P("seq", "head"), P("seq", "head"), P("seq", "head"), P("head"), P("seq", "head"))
    return jax.shard_map(
        local,
        mesh=mesh,
        in_specs=placed,
        out_specs=(P("seq", "head"), P("seq", "head"), P("seq", "head"), P("seq", "head")),
        check_vma=False,
    )
```

```python
import functools

import jax
import jax.numpy as jnp
from jax import lax
from jax.experimental import pallas as pl
from jax.experimental.pallas import tpu as pltpu
from jax.sharding import PartitionSpec as P

HD = 128
BLK = 512
NY = 4
CHUNKS = 4
ORDER = (1, 2, 0, 3)
ARRIVAL = (1, 2, 0, 3)
AHEAD = (3, 3)
BEHIND = (2, 2, 2)
HALF = BLK // 2
F32 = jnp.float32
BF16 = jnp.bfloat16
MESH = pl.DeviceIdType.MESH


def dot_nn(a, b):
    return lax.dot_general(a, b, (((1,), (0,)), ((), ())), preferred_element_type=F32)


def dot_nt(a, b):
    return lax.dot_general(a, b, (((1,), (1,)), ((), ())), preferred_element_type=F32)


def dot_tn(a, b):
    return lax.dot_general(a, b, (((0,), (0,)), ((), ())), preferred_element_type=F32)


def split(a, count):
    parts = []
    for _ in range(count):
        parts.append(a.astype(BF16))
        a = a - parts[-1].astype(F32)
    return parts


def far_first(count):
    return sorted(range(1, count), key=lambda d: -min(d, count - d))


class Scan:
    def __init__(self, nz, rows, reverse, refs, sems):
        self.nz, self.rows, self.reverse = nz, rows, reverse
        self.block, self.b1, self.tot, self.b2, self.pre, self.b3, self.ret, self.b4 = refs[:8]
        self.a1, self.a2, self.a3, self.a4, self.a5 = refs[8:]
        self.ysend, self.yrecv, self.zsend, self.zrecv = sems
        seq = lax.axis_index("seq")
        self.head = lax.axis_index("head")
        self.z, self.y = lax.div(seq, NY), lax.rem(seq, NY)
        self.quarter = rows // NY
        self.piece = self.quarter // nz
        self.sends = []

    def y_copy(self, phase, c, d, src, dst):
        k = (phase * CHUNKS + c) * (NY - 1) + d - 1
        to = self.z * NY + lax.rem(self.y + d, NY)
        return pltpu.make_async_remote_copy(
            src_ref=src, dst_ref=dst, send_sem=self.ysend.at[k], recv_sem=self.yrecv.at[k],
            device_id=(to, self.head), device_id_type=MESH,
        )

    def z_copy(self, phase, c, d, src, dst):
        k = (phase * CHUNKS + c) * (self.nz - 1) + d - 1
        to = lax.rem(self.z + d, self.nz) * NY + self.y
        return pltpu.make_async_remote_copy(
            src_ref=src, dst_ref=dst, send_sem=self.zsend.at[k], recv_sem=self.zrecv.at[k],
            device_id=(to, self.head), device_id_type=MESH,
        )

    def begin(self, copies):
        for copy in copies:
            copy.start()
        self.sends += copies
        return copies

    def y_out(self, c):
        base = c * self.rows

        def part(q):
            return self.block.at[pl.ds(pl.multiple_of(base + q * self.quarter, 8), self.quarter)]

        copies = self.begin([
            self.y_copy(0, c, d, part(lax.rem(self.y + d, NY)), self.b1.at[c, self.y]) for d in (2, 1, 3)
        ])
        self.b1[c, self.y] = part(self.y)[...]
        return copies

    def z_out(self, c, arriving):
        for copy in arriving:
            copy.wait_recv()
        self.tot[c] = (self.b1[c, 0] + self.b1[c, 1]) + (self.b1[c, 2] + self.b1[c, 3])

        def part(j):
            return self.tot.at[c, pl.ds(pl.multiple_of(j * self.piece, 8), self.piece)]

        copies = self.begin([
            self.z_copy(0, c, d, part(lax.rem(self.z + d, self.nz)), self.b2.at[c, self.z]) for d in far_first(self.nz)
        ])
        self.b2[c, self.z] = part(self.z)[...]
        return copies

    def z_back(self, c, arriving):
        for copy in arriving:
            copy.wait_recv()
        order = range(self.nz)
        total = jnp.zeros((self.piece, HD), F32)
        for j in reversed(order) if self.reverse else order:
            self.pre[c, j] = total
            total = total + self.b2[c, j]
        copies = self.begin([
            self.z_copy(1, c, d, self.pre.at[c, lax.rem(self.z + d, self.nz)], self.b3.at[c, self.z]) for d in far_first(self.nz)
        ])
        self.b3[c, self.z] = self.pre[c, self.z]
        return copies

    def y_back(self, c, arriving):
        for copy in arriving:
            copy.wait_recv()
        total = self.b3[c].reshape(self.quarter, HD)
        order = range(NY)
        for j in reversed(order) if self.reverse else order:
            self.ret[c, j] = total
            total = total + self.b1[c, j]
        copies = self.begin([
            self.y_copy(1, c, d, self.ret.at[c, lax.rem(self.y + d, NY)], self.b4.at[c, self.y]) for d in (2, 1, 3)
        ])
        self.b4[c, self.y] = self.ret[c, self.y]
        return copies

    def a_out(self):
        height = self.rows // self.nz

        def part(j):
            return self.block.at[pl.ds(pl.multiple_of(j * height, 8), height)]

        copies = self.begin([
            self.z_copy(0, 0, d, part(lax.rem(self.z + d, self.nz)), self.a1.at[self.z]) for d in far_first(self.nz)
        ])
        self.a1[self.z] = part(self.z)[...]
        return copies

    def a_mid(self, arriving):
        for copy in arriving:
            copy.wait_recv()
        height = self.rows // self.nz // NY

        def part(q):
            return self.a1.at[:, pl.ds(pl.multiple_of(q * height, 8), height)]

        copies = self.begin([
            self.y_copy(0, 0, d, part(lax.rem(self.y + d, NY)), self.a2.at[self.y]) for d in (2, 1, 3)
        ])
        self.a2[self.y] = part(self.y)[...]
        return copies

    def a_back(self, arriving):
        for copy in arriving:
            copy.wait_recv()
        order = [(j, i) for j in range(self.nz) for i in range(NY)]
        total = jnp.zeros(self.a2.shape[2:], F32)
        for j, i in reversed(order) if self.reverse else order:
            self.a3[i, j] = total
            total = total + self.a2[i, j]
        copies = self.begin([
            self.y_copy(1, 0, d, self.a3.at[lax.rem(self.y + d, NY)], self.a4.at[self.y]) for d in (2, 1, 3)
        ])
        self.a4[self.y] = self.a3[self.y]
        return copies

    def a_end(self, arriving):
        for copy in arriving:
            copy.wait_recv()
        copies = self.begin([
            self.z_copy(1, 0, d, self.a4.at[:, lax.rem(self.z + d, self.nz)], self.a5.at[self.z])
            for d in far_first(self.nz)
        ])
        self.a5[self.z] = self.a4[:, self.z]
        return copies

    def first(self, c):
        return self.a_out() if c == 0 else self.y_out(c)

    def second(self, moving):
        for c in (1, 2, 0, 3):
            moving[c] = self.a_mid(moving[c]) if c == 0 else self.z_out(c, moving[c])

    def third(self, moving):
        for c in (0, 1, 2, 3):
            moving[c] = self.a_back(moving[c]) if c == 0 else self.z_back(c, moving[c])

    def fourth(self, moving):
        for c in (0, 1, 2, 3):
            moving[c] = self.a_end(moving[c]) if c == 0 else self.y_back(c, moving[c])

    def result(self, c, arriving):
        for copy in arriving:
            copy.wait_recv()
        return (self.a5[...] if c == 0 else self.b4[c]).reshape(self.rows, HD).astype(BF16)

    def finish(self):
        for copy in self.sends:
            copy.wait_send()


def lanes(h):
    return pl.ds(pl.multiple_of(h * HD, HD), HD)


def sub(h):
    return pl.ds(pl.multiple_of(h * HD, HD), HD)


def each(first, count, body):
    def step(h, _):
        body(h)
        return 0

    lax.fori_loop(first, first + count, step, 0)


def kernel(nz, nh, heads, q_hbm, k_hbm, v_hbm, gain_hbm, g_hbm, normed, qgrad, kgrad, vgrad, kpart_end, vpart_end,
           later_end, k_end, v_end, q, k, v, gain, g, grad_norm, scores, att, dout, kpart, vpart, state_bf, squares,
           products, inv_b, coef_b, head_src, head_dst, *rest):
    fwd_refs, bwd_refs = rest[0:13], rest[13:26]
    fwd_sems, bwd_sems = rest[26:30], rest[30:34]
    in_sem, head_send, head_recv = rest[34:37]
    scale = HD ** (-0.5)
    per = heads // CHUNKS
    rows = per * HD
    width = heads * HD
    seq, head = lax.axis_index("seq"), lax.axis_index("head")
    z, y = lax.div(seq, NY), lax.rem(seq, NY)

    loads = []

    def load(c):
        cols = pl.ds(c * rows, rows)
        pair = []
        for i, (src, dst) in enumerate(((k_hbm, k), (v_hbm, v))):
            copy = pltpu.make_async_copy(src.at[:, cols], dst.at[:, cols], in_sem.at[2 * c + i])
            copy.start()
            pair.append(copy)
        loads.append(pair)

    load(0)
    barrier = pltpu.get_barrier_semaphore()
    for d in far_first(nz):
        to = lax.rem(z + d, nz) * NY + y
        pl.semaphore_signal(barrier, inc=1, device_id=(to, head), device_id_type=MESH)
    for d in range(1, nh):
        pl.semaphore_signal(barrier, inc=1, device_id=(seq, lax.rem(head + d, nh)), device_id_type=MESH)
    for d in far_first(NY):
        to = z * NY + lax.rem(y + d, NY)
        pl.semaphore_signal(barrier, inc=1, device_id=(to, head), device_id_type=MESH)

    for c in range(1, CHUNKS):
        load(c)
    late = []
    for i, (src, dst) in enumerate(((q_hbm, q), (g_hbm, g), (gain_hbm, gain))):
        copy = pltpu.make_async_copy(src, dst, in_sem.at[2 * CHUNKS + i])
        copy.start()
        late.append(copy)

    fwd = Scan(nz, rows, False, fwd_refs, fwd_sems)
    bwd = Scan(nz, rows, True, bwd_refs, bwd_sems)

    def kv(h):
        fwd.block[sub(h), :] = dot_tn(k[:, lanes(h)], v[:, lanes(h)])

    moving = []
    for c in range(CHUNKS):
        for copy in loads[c]:
            copy.wait()
        for h in range(c * per, (c + 1) * per):
            kv(h)
        if c == 0:
            pl.semaphore_wait(barrier, (NY - 1) + (nz - 1) + (nh - 1))
        moving.append(fwd.first(c))
    for copy in late:
        copy.wait()

    causal = lax.broadcasted_iota(jnp.int32, (HALF, HALF), 0) >= lax.broadcasted_iota(jnp.int32, (HALF, HALF), 1)

    def tiles(a, b, factor):
        top = jnp.where(causal, dot_nt(a[:HALF], b[:HALF]) * factor, 0.0).astype(BF16)
        low = (dot_nt(a[HALF:], b[:HALF]) * factor).astype(BF16)
        end = jnp.where(causal, dot_nt(a[HALF:], b[HALF:]) * factor, 0.0).astype(BF16)
        return top, low, end

    def intra(h):
        vh = v[:, lanes(h)]
        top, low, end = tiles(q[:, lanes(h)], k[:, lanes(h)], scale)
        scores[h, 0], scores[h, 1], scores[h, 2] = top, low, end
        att[:HALF, lanes(h)] = dot_nn(top, vh[:HALF])
        att[HALF:, lanes(h)] = dot_nn(low, vh[:HALF]) + dot_nn(end, vh[HALF:])
        grad_norm[:, lanes(h)] = g[:, lanes(h)].astype(F32) * gain[:, lanes(h)]

    each(0, AHEAD[0], intra)
    fwd.second(moving)
    each(AHEAD[0], AHEAD[1], intra)
    fwd.third(moving)
    each(AHEAD[0] + AHEAD[1], heads - AHEAD[0] - AHEAD[1], intra)
    fwd.fourth(moving)
    for c in ARRIVAL:
        here = fwd.result(c, moving[c])
        state_bf[pl.ds(c * rows, rows), :] = here
        sq, pr = (0.0, 0.0) if c == ARRIVAL[0] else (squares[...], products[...])
        for i in range(per):
            h = c * per + i
            a = att[:, lanes(h)] + scale * dot_nn(q[:, lanes(h)], here[i * HD : (i + 1) * HD])
            att[:, lanes(h)] = a
            sq = sq + a * a
            pr = pr + a * grad_norm[:, lanes(h)]
        if c != ARRIVAL[-1]:
            squares[...], products[...] = sq, pr

    row = lax.broadcasted_iota(jnp.int32, (8, HD), 0)
    groups = BLK // HD
    packed = jnp.zeros((8, HD), F32)
    for t in range(groups):
        for first, totals in ((0, sq), (groups, pr)):
            pick = (row == first + t).astype(BF16)
            packed = packed + dot_nt(
                jnp.concatenate([pick, pick], axis=1), jnp.concatenate(split(totals[t * HD : (t + 1) * HD], 2), axis=1)
            )
    head_src[...] = packed
    head_copies = []
    for d in far_first(nh):
        copy = pltpu.make_async_remote_copy(
            src_ref=head_src, dst_ref=head_dst.at[head], send_sem=head_send.at[d - 1], recv_sem=head_recv.at[d - 1],
            device_id=(seq, lax.rem(head + d, nh)), device_id_type=MESH,
        )
        copy.start()
        head_copies.append(copy)
    head_dst[head] = packed
    for copy in head_copies:
        copy.wait_recv()
    sums = head_dst[0]
    for j in range(1, nh):
        sums = sums + head_dst[j]
    full = nh * width
    inv = 1.0 / jnp.sqrt(sums[:groups] / full + 1e-06)
    proj = (sums[groups:] * inv) / full
    both = jnp.concatenate(split(jnp.concatenate([inv, (inv * proj) * inv], axis=0), 3), axis=0)
    for t in range(groups):
        part = pl.ds(t * HD, HD)
        for first, spread in ((0, inv_b), (groups, coef_b)):
            pick = (row == first + t).astype(BF16)
            spread[part, :] = dot_tn(both, jnp.concatenate([pick, pick, pick], axis=0))

    def grad(h):
        d = (grad_norm[:, lanes(h)] * inv_b[...] - att[:, lanes(h)] * coef_b[...]).astype(BF16)
        dout[:, lanes(h)] = d
        bwd.block[sub(h), :] = dot_tn(q[:, lanes(h)], d)

    for c in range(CHUNKS):
        for h in range(c * per, (c + 1) * per):
            grad(h)
        moving[c] = bwd.first(c)

    def back(h):
        qh, kh, vh, d = q[:, lanes(h)], k[:, lanes(h)], v[:, lanes(h)], dout[:, lanes(h)]
        normed[:, lanes(h)] = (att[:, lanes(h)] * inv_b[...] * gain[:, lanes(h)]).astype(BF16)
        top, low, end = tiles(d, vh, 1.0)
        carried = dot_nt(d, state_bf[sub(h), :])
        qgrad[:HALF, lanes(h)] = (scale * (dot_nn(top, kh[:HALF]) + carried[:HALF])).astype(BF16)
        qgrad[HALF:, lanes(h)] = (
            scale * (dot_nn(low, kh[:HALF]) + dot_nn(end, kh[HALF:]) + carried[HALF:])
        ).astype(BF16)
        kpart[:HALF, lanes(h)] = dot_tn(top, qh[:HALF]) + dot_tn(low, qh[HALF:])
        kpart[HALF:, lanes(h)] = dot_tn(end, qh[HALF:])
        vpart[:HALF, lanes(h)] = dot_tn(scores[h, 0], d[:HALF]) + dot_tn(scores[h, 1], d[HALF:])
        vpart[HALF:, lanes(h)] = dot_tn(scores[h, 2], d[HALF:])

    done = 0
    each(done, BEHIND[0], back)
    done += BEHIND[0]
    bwd.second(moving)
    each(done, BEHIND[1], back)
    done += BEHIND[1]
    bwd.third(moving)
    each(done, BEHIND[2], back)
    done += BEHIND[2]
    early, bwd.sends = bwd.sends, []
    bwd.fourth(moving)
    each(done, heads - done, back)
    fwd.finish()
    for copy in head_copies + early:
        copy.wait_send()
    end = pl.ds((CHUNKS - 1) * rows, rows)
    k_end[...], v_end[...] = k[:, end], v[:, end]
    kpart_end[...], vpart_end[...] = kpart[:, end], vpart[:, end]
    for c in ARRIVAL:
        here = bwd.result(c, moving[c])
        if c == CHUNKS - 1:
            later_end[...] = here
            break
        for i in range(per):
            h = c * per + i
            one = here[i * HD : (i + 1) * HD]
            kgrad[:, lanes(h)] = (scale * (kpart[:, lanes(h)] + dot_nt(v[:, lanes(h)], one))).astype(BF16)
            vgrad[:, lanes(h)] = (vpart[:, lanes(h)] + scale * dot_nn(k[:, lanes(h)], one)).astype(BF16)

    bwd.finish()


def finish_kernel(per, normed, qgrad, kgrad, vgrad, kpart, vpart, later, k, v, normed_hbm, qgrad_hbm, kgrad_hbm,
                  vgrad_hbm, kgrad_end, vgrad_end, out_sem):
    scale = HD ** (-0.5)
    outs = []

    def put(src, dst):
        copy = pltpu.make_async_copy(src, dst, out_sem.at[len(outs)])
        copy.start()
        outs.append(copy)

    begun = kgrad.shape[1] - per * HD
    for src, dst in ((kgrad, kgrad_hbm), (vgrad, vgrad_hbm)):
        put(src.at[:, pl.ds(0, begun)], dst.at[:, pl.ds(0, begun)])
    put(normed, normed_hbm)
    put(qgrad, qgrad_hbm)
    for h in range(per):
        kgrad_end[:, lanes(h)] = (scale * (kpart[:, lanes(h)] + dot_nt(v[:, lanes(h)], later[sub(h), :]))).astype(BF16)
        vgrad_end[:, lanes(h)] = (vpart[:, lanes(h)] + scale * dot_nn(k[:, lanes(h)], later[sub(h), :])).astype(BF16)
    for src, dst in ((kgrad_end, kgrad_hbm), (vgrad_end, vgrad_hbm)):
        put(src, dst.at[:, pl.ds(begun, per * HD)])
    for copy in outs:
        copy.wait()


def local(queries, keys, values, norm_gain, out_grad):
    blk, width = queries.shape
    heads = width // HD
    nz = lax.axis_size("seq") // NY
    nh = lax.axis_size("head")
    rows = heads // CHUNKS * HD
    quarter = rows // NY
    piece = quarter // nz
    vmem = pltpu.VMEM

    def scan_refs():
        return [
            vmem((heads * HD, HD), F32),
            vmem((CHUNKS, NY, quarter, HD), F32),
            vmem((CHUNKS, quarter, HD), F32),
            vmem((CHUNKS, nz, piece, HD), F32),
            vmem((CHUNKS, nz, piece, HD), F32),
            vmem((CHUNKS, nz, piece, HD), F32),
            vmem((CHUNKS, NY, quarter, HD), F32),
            vmem((CHUNKS, NY, quarter, HD), F32),
            vmem((nz, rows // nz, HD), F32),
            vmem((NY, nz, rows // nz // NY, HD), F32),
            vmem((NY, nz, rows // nz // NY, HD), F32),
            vmem((NY, nz, rows // nz // NY, HD), F32),
            vmem((nz, NY, rows // nz // NY, HD), F32),
        ]

    def scan_sems():
        y, zz = 2 * CHUNKS * (NY - 1), 2 * CHUNKS * (nz - 1)
        dma = pltpu.SemaphoreType.DMA
        return [dma((y,)), dma((y,)), dma((zz,)), dma((zz,))]

    big_f32, big_bf16 = vmem((blk, width), F32), vmem((blk, width), BF16)
    end_f32, end_bf16 = vmem((blk, rows), F32), vmem((blk, rows), BF16)
    scratch = [
        big_bf16, big_bf16, big_bf16, vmem((1, width), F32), big_bf16, big_f32,
        vmem((heads, 3, HALF, HALF), BF16),
        big_f32, big_bf16, big_f32, big_f32,
        vmem((heads * HD, HD), BF16),
        vmem((blk, HD), F32), vmem((blk, HD), F32), vmem((blk, HD), F32), vmem((blk, HD), F32),
        vmem((8, HD), F32), vmem((nh, 8, HD), F32),
        *scan_refs(), *scan_refs(), *scan_sems(), *scan_sems(),
        pltpu.SemaphoreType.DMA((2 * CHUNKS + 3,)),
        pltpu.SemaphoreType.DMA((nh - 1,)),
        pltpu.SemaphoreType.DMA((nh - 1,)),
    ]
    out = jax.ShapeDtypeStruct((blk, width), BF16)
    anywhere, in_vmem = pl.BlockSpec(memory_space=pl.ANY), pl.BlockSpec(memory_space=pltpu.VMEM)
    parts = pl.pallas_call(
        functools.partial(kernel, nz, nh, heads),
        out_shape=(
            big_bf16, big_bf16, big_bf16, big_bf16, end_f32, end_f32, vmem((rows, HD), BF16), end_bf16, end_bf16,
        ),
        in_specs=[anywhere] * 5,
        out_specs=(in_vmem,) * 9,
        scratch_shapes=scratch,
        compiler_params=pltpu.CompilerParams(
            collective_id=0, has_side_effects=True, vmem_limit_bytes=40 * 1024 * 1024
        ),
        name="linear_attention",
    )(*[
        pltpu.with_memory_space_constraint(a, pltpu.HBM)
        for a in (queries, keys, values, norm_gain.reshape(1, width), out_grad)
    ])
    return pl.pallas_call(
        functools.partial(finish_kernel, heads // CHUNKS),
        out_shape=(out,) * 4,
        in_specs=[in_vmem] * 9,
        out_specs=(anywhere,) * 4,
        scratch_shapes=[end_bf16, end_bf16, pltpu.SemaphoreType.DMA((6,))],
        compiler_params=pltpu.CompilerParams(vmem_limit_bytes=28 * 1024 * 1024),
        name="key_value_grads",
    )(*parts)


def solution(mesh):
    placed = (P("seq", "head"), P("seq", "head"), P("seq", "head"), P("head"), P("seq", "head"))
    return jax.shard_map(
        local,
        mesh=mesh,
        in_specs=placed,
        out_specs=(P("seq", "head"), P("seq", "head"), P("seq", "head"), P("seq", "head")),
        check_vma=False,
    )
```
